32 devices in a mesh: tok: 16 (over z, x, core), mem: 2 (over y).
Axes of the slice: x: 2, y: 2, z: 4, core: 2. Of those that a mesh axis runs over, the one named last changes fastest.
Arguments:
- tokens: bfloat16 [6144, 1472], P(('tok', 'mem')), may hold values from -6 to 6
- memory: bfloat16 [9216, 1472], P(('tok', 'mem')), may hold values from -6 to 6
- target_lengths: int32 [16, 2, 8], P('tok'), may hold values from 1 to 69, 192 in all within a row
- memory_lengths: int32 [16, 16], P('tok'), may hold values from 1 to 384, 576 in all within a row
- keep_mask: int32 [9216], P(('tok', 'mem')), may hold values 0 or 1
- distance_bucket_lookup: int32 [192], replicated, may hold values from 0 to 31, as said below
- self_query: bfloat16 [1472, 384], P(None, ('tok', 'mem')), may hold values from -0.0390625 to 0.0390625
- self_kv: bfloat16 [2, 1472, 384], P(None, None, ('tok', 'mem')), may hold values from -0.15625 to 0.15625
- self_out: bfloat16 [384, 1472], P(('tok', 'mem')), may hold values from -0.625 to 0.625
- cross_query: bfloat16 [1472, 384], P(None, ('tok', 'mem')), may hold values from -0.0390625 to 0.0390625
- cross_key_value: bfloat16 [2, 1472, 384], P(None, None, ('tok', 'mem')), may hold values from -0.15625 to 0.15625
- cross_out: bfloat16 [384, 1472], P(('tok', 'mem')), may hold values from -0.625 to 0.625
- ffn_in: bfloat16 [2, 1472, 3584], P(None, None, ('tok', 'mem')), may hold values from -0.15625 to 0.15625
- ffn_down: bfloat16 [3584, 1472], P(('tok', 'mem')), may hold values from -0.09375 to 0.09375
- norm_gains: float32 [3, 1472], replicated, may hold values from 0.5 to 1.5
- rel_bias: float32 [32, 6], replicated, may hold values from -4 to 4
- cotangent: bfloat16 [6144, 1472], P(('tok', 'mem')), may hold values from -6 to 6
Outputs:
- block_out: bfloat16 [6144, 1472], P(('tok', 'mem'))
- input_grad: float32 [6144, 1472], P(('tok', 'mem'))
- memory_grad: float32 [9216, 1472], P(('tok', 'mem'))
- self_query_grad: float32 [1472, 384], P(None, ('tok', 'mem'))
- self_kv_grad: float32 [2, 1472, 384], P(None, None, ('tok', 'mem'))
- self_out_grad: float32 [384, 1472], P(('tok', 'mem'))
- cross_query_grad: float32 [1472, 384], P(None, ('tok', 'mem'))
- cross_kv_grad: float32 [2, 1472, 384], P(None, None, ('tok', 'mem'))
- cross_out_grad: float32 [384, 1472], P(('tok', 'mem'))
- ffn_in_grad: float32 [2, 1472, 3584], P(None, None, ('tok', 'mem'))
- ffn_down_grad: float32 [3584, 1472], P(('tok', 'mem'))
- gain_grads: float32 [3, 1472], replicated
- rel_bias_grad: float32 [32, 6], replicated
The draws below stay inside these ranges and needn't reach their ends.
Inputs may be any that keep to these rules, and one draw needn't show every extreme that they name: Every block of target_lengths sums to 192. Every row of memory_lengths sums to 576. distance_bucket_lookup[d] equals d for d < 16, never falls as d grows, and equals 31 from d = 68 on.
All inputs are finite; a program needn't handle non-finite values. No bound on the sum of `keep_mask` on one device may be relied on, other than what follows from the above.
Results may differ from the reference program's by a relative error of at most 0.024.
Values may be sent and summed in bfloat16 or wider, within the bound.
No kernel may reach another device: no remote copies, remote signals or barrier semaphores. Data moves between devices by JAX's collectives and lax.ppermute only.
A program may use at most 320 MiB of HBM per device.

```python
import math
import jax
import jax.numpy as jnp
import numpy as np
from jax import lax

D = 1472
HEADS = 6
HEAD_DIM = 64
FF = 3584
BUCKETS = 32
TOK_DEV = 192
ITEMS_DEV = 8
INNER = 384
MEMORY_PER_UNIT = 288
MEM_MOST = 384
TGT_MOST = 69
TOKENS = 6144
MEMROWS = 9216
N_TOK = 16
N_MEM = 2


def draw_distance_bucket_lookup(key, part):
    limits = jax.random.randint(key, (BUCKETS // 2 - 1,), BUCKETS // 2 + 1, TGT_MOST)
    distance = jnp.arange(TOK_DEV, dtype=jnp.int32)
    beyond = jnp.sum((distance[:, None] >= limits[None, :]).astype(jnp.int32), axis=1)
    return jnp.where(distance < BUCKETS // 2, distance, BUCKETS // 2 + beyond).astype(jnp.int32)


def place_ends(values, own_key, smallest, high):
    extent = values.shape
    index_at = [jax.random.randint(jax.random.fold_in(own_key, axis), (), 0, extent[axis]) for axis in range(len(extent))]
    values = values.at[tuple(index_at)].set(smallest)
    longest = extent.index(max(extent))
    index_at[longest] = (index_at[longest] + 1) % extent[longest]
    return values.at[tuple(index_at)].set(high)


def block_scale(stream_key, dims, cuts, least, high):
    gain, own = 1.0, jax.random.fold_in(stream_key, 6)
    for axis_at, blocks in cuts:
        draws = jnp.exp(jax.random.uniform(jax.random.fold_in(own, axis_at), (blocks,), jnp.float32, least / len(cuts), high / len(cuts)))
        gain = gain * jnp.repeat(draws, dims[axis_at] // blocks).reshape([-1 if axis == axis_at else 1 for axis in range(len(dims))])
    return gain


def length_profile(number_of, total, bound, lean):
    portions = [(1 << 20) // math.isqrt(grade ** lean) + 1 for grade in range(2, number_of + 1)]
    rest, given = total - bound - (number_of - 1), [1] * (number_of - 1)
    while rest > 0:
        candidates = [i for i in range(number_of - 1) if given[i] < bound]
        whole, left = sum([portions[i] for i in candidates]), rest
        for i in candidates:
            more = min(bound - given[i], max(1, left * portions[i] // whole), rest)
            given[i] = given[i] + more
            rest = rest - more
    return np.array([bound] + given)


def uneven(rng, count, total, reach, skew):
    if count == 2:
        one = jax.random.randint(rng, (), max(1, total - reach), min(reach, total - 1) + 1)
        return jnp.stack([one, total - one])
    lengths = jnp.asarray(length_profile(count, total, reach, skew), jnp.int32)
    twos = (count - 1) // 2
    source_of, sink = lengths[1:1 + 2 * twos:2], lengths[2:2 + 2 * twos:2]
    margin = jnp.minimum(source_of - 1, reach - sink)
    shifted = jax.random.randint(jax.random.fold_in(rng, 1), (twos,), 0, 1 << 20) % (margin + 1)
    lengths = lengths.at[1:1 + 2 * twos:2].set(source_of - shifted).at[2:2 + 2 * twos:2].set(sink + shifted)
    return lengths[jax.random.permutation(jax.random.fold_in(rng, 2), count)]


def gaussian(own_key, dims, deviation, most, cuts=(), kind=jnp.bfloat16):
    array = deviation * jax.random.normal(own_key, dims, jnp.float32)
    if cuts:
        array = array * block_scale(own_key, dims, cuts, -0.22, 0.18)
    return jnp.clip(array, -most, most).astype(kind)


def setup_inputs(seed: int = 0) -> dict:
    seeds = jax.random.split(jax.random.key(seed), 18)
    tokens = gaussian(seeds[0], (TOKENS, D), 1.0, 6.0, ((0, 32),))
    memory = gaussian(seeds[1], (MEMROWS, D), 1.0, 6.0, ((0, 32),))
    target_lengths = jax.vmap(lambda own: uneven(own, ITEMS_DEV, TOK_DEV, TGT_MOST, 2))(jax.random.split(seeds[2], N_TOK * N_MEM)).reshape((N_TOK, N_MEM, ITEMS_DEV)).astype(jnp.int32)
    memory_lengths = jax.vmap(lambda own: uneven(own, N_MEM * ITEMS_DEV, N_MEM * MEMORY_PER_UNIT, MEM_MOST, 2))(jax.random.split(seeds[3], N_TOK)).reshape((N_TOK, N_MEM * ITEMS_DEV)).astype(jnp.int32)
    keep_mask = place_ends((jax.random.randint(seeds[4], (MEMROWS,), 0, 2) < 1).astype(jnp.int32), jax.random.fold_in(seeds[4], 1), 0, 1)
    distance_bucket_lookup = draw_distance_bucket_lookup(jax.random.fold_in(seeds[17], 71), 0)
    self_query = gaussian(seeds[6], (D, INNER), (16 * D) ** -0.5, 0.0390625, ((1, 32),))
    self_kv = gaussian(seeds[7], (2, D, INNER), D ** -0.5, 0.15625, ((2, 32),))
    self_out = gaussian(seeds[8], (INNER, D), (INNER // 4) ** -0.5, 0.625, ((0, 32),))
    cross_query = gaussian(seeds[9], (D, INNER), (16 * D) ** -0.5, 0.0390625, ((1, 32),))
    cross_key_value = gaussian(seeds[10], (2, D, INNER), D ** -0.5, 0.15625, ((2, 32),))
    cross_out = gaussian(seeds[11], (INNER, D), (INNER // 4) ** -0.5, 0.625, ((0, 32),))
    ffn_in = gaussian(seeds[12], (2, D, FF), D ** -0.5, 0.15625, ((2, 32),))
    ffn_down = gaussian(seeds[13], (FF, D), FF ** -0.5, 0.09375, ((0, 32),))
    norm_gains = jnp.clip(1.0 + 0.1 * jax.random.normal(seeds[14], (3, D), jnp.float32), 0.5, 1.5)
    rel_bias = gaussian(seeds[15], (BUCKETS, HEADS), 1.0, 4.0, (), jnp.float32)
    cotangent = gaussian(seeds[16], (TOKENS, D), 1.0, 6.0, ((0, 32),))
    return dict(tokens=tokens, memory=memory, target_lengths=target_lengths, memory_lengths=memory_lengths, keep_mask=keep_mask, distance_bucket_lookup=distance_bucket_lookup, self_query=self_query, self_kv=self_kv, self_out=self_out, cross_query=cross_query, cross_key_value=cross_key_value, cross_out=cross_out, ffn_in=ffn_in, ffn_down=ffn_down, norm_gains=norm_gains, rel_bias=rel_bias, cotangent=cotangent)


eps = 1e-06
masked_value = -1e+30
highest = lax.Precision.HIGHEST

@jax.custom_vjp
def low(v):
    return lax.optimization_barrier(v.astype(jnp.bfloat16)).astype(jnp.float32)

@jax.custom_vjp
def low_back(v):
    return v

def low_keep(v):
    return (low(v), None)

def low_pass(kept, grad):
    return (grad,)

def back_keep(v):
    return (v, None)

def back_low(kept, grad):
    return (low(grad),)
low.defvjp(low_keep, low_pass)
low_back.defvjp(back_keep, back_low)

def product(left, right):
    return jnp.dot(left, right, precision=highest, preferred_element_type=jnp.float32)

def rms_norm(values, norm_gain):
    norm_scale = lax.rsqrt(lax.optimization_barrier(jnp.mean(values * values, axis=-1, keepdims=True)) + eps)
    return values * norm_scale * norm_gain

def run_items(run_lengths, row_count):
    run_ends = jnp.cumsum(run_lengths).astype(jnp.int32)
    position = jnp.arange(row_count, dtype=jnp.int32)
    return lax.optimization_barrier(jnp.sum((position[:, None] >= run_ends[None, :]).astype(jnp.int32), axis=1)).astype(jnp.int32)

def split_heads(matrix):
    return matrix.reshape(matrix.shape[0], HEADS, HEAD_DIM).transpose(1, 0, 2)

def merge_heads(mixed):
    return mixed.transpose(1, 0, 2).reshape(mixed.shape[1], HEADS * HEAD_DIM)

def group_layer(weights, x_first, memory_rows, target_runs, memory_runs, keep_rows, distance_bucket_lookup):
    self_query, self_kv, self_out, cross_query, cross_key_value, cross_out, ffn_in, ffn_down, norm_gains, rel_bias = weights
    row_count = x_first.shape[0]
    slot_count = memory_rows.shape[0]
    block_items = [run_items(target_runs[block_index], TOK_DEV) + block_index * ITEMS_DEV for block_index in range(N_MEM)]
    row_items = jnp.concatenate(block_items)
    position = jnp.arange(row_count, dtype=jnp.int32)
    offset = position[:, None] - position[None, :]
    allowed = (row_items[:, None] == row_items[None, :]) & (offset >= 0)
    distance = jnp.clip(offset, 0, TOK_DEV - 1)
    bias_heads = jnp.transpose(rel_bias[distance_bucket_lookup[distance]], (2, 0, 1))
    normed_one = low(rms_norm(x_first, norm_gains[0]))
    query_self = low_back(low(product(normed_one, self_query)))
    key_self = low_back(low(product(normed_one, self_kv[0])))
    value_self = low_back(low(product(normed_one, self_kv[1])))
    raw_self = low_back(jnp.einsum('hid,hjd->hij', split_heads(query_self), split_heads(key_self), precision=highest))
    probs_self = jax.nn.softmax(jnp.where(allowed[None], raw_self + bias_heads, masked_value), axis=-1)
    mixed_self = jnp.einsum('hij,hjd->hid', low(probs_self), split_heads(value_self), precision=highest)
    attn_low = low_back(low(merge_heads(mixed_self)))
    x_second = x_first + low_back(product(attn_low, self_out))
    slot_position = jnp.arange(slot_count, dtype=jnp.int32)
    run_ends = jnp.cumsum(memory_runs).astype(jnp.int32)
    run_starts = run_ends - memory_runs
    slot_items = lax.optimization_barrier(jnp.sum((slot_position[:, None] >= run_ends[None, :]).astype(jnp.int32), axis=1))
    first_slot = jnp.any(slot_position[:, None] == run_starts[None, :], axis=1)
    live_slot = (keep_rows > 0) | first_slot
    reachable = (row_items[:, None] == slot_items[None, :]) & live_slot[None, :]
    normed_two = low(rms_norm(x_second, norm_gains[1]))
    query_cross = low_back(low(product(normed_two, cross_query)))
    key_cross = low_back(low(product(memory_rows, cross_key_value[0])))
    cross_value_rows = low_back(low(product(memory_rows, cross_key_value[1])))
    raw_cross = low_back(jnp.einsum('hid,hjd->hij', split_heads(query_cross), split_heads(key_cross), precision=highest))
    probs_cross = jax.nn.softmax(jnp.where(reachable[None], raw_cross, masked_value), axis=-1)
    mixed_cross = jnp.einsum('hij,hjd->hid', probs_cross, split_heads(cross_value_rows), precision=highest)
    cross_low = low_back(low(merge_heads(mixed_cross)))
    hidden_third = x_second + low_back(product(cross_low, cross_out))
    normed_three = low(rms_norm(hidden_third, norm_gains[2]))
    gate_pre = low_back(product(normed_three, ffn_in[0]))
    up_pre = low_back(product(normed_three, ffn_in[1]))
    hidden = low(jax.nn.gelu(gate_pre, approximate=True) * up_pre)
    return hidden_third + low_back(product(hidden, ffn_down))

def reference(tokens, memory, target_lengths, memory_lengths, keep_mask, distance_bucket_lookup, self_query, self_kv, self_out, cross_query, cross_key_value, cross_out, ffn_in, ffn_down, norm_gains, rel_bias, cotangent):
    weights = tuple((weight.astype(jnp.float32) for weight in (self_query, self_kv, self_out, cross_query, cross_key_value, cross_out, ffn_in, ffn_down, norm_gains, rel_bias)))
    group_rows = N_MEM * TOK_DEV
    group_slots = N_MEM * MEMORY_PER_UNIT
    x_groups = tokens.astype(jnp.float32).reshape(N_TOK, group_rows, D)
    memory_groups = memory.astype(jnp.float32).reshape(N_TOK, group_slots, D)
    keep_groups = keep_mask.reshape(N_TOK, group_slots)
    checked = jax.checkpoint(group_layer)

    def forward(weight_set, x_all, memory_all):

        def one_group(pieces):
            return checked(weight_set, pieces[0], pieces[1], pieces[2], pieces[3], pieces[4], distance_bucket_lookup)
        return lax.map(one_group, (x_all, memory_all, target_lengths, memory_lengths, keep_groups))
    block_groups, pullback = jax.vjp(forward, weights, x_groups, memory_groups)
    weight_grads, x_grads, memory_grads = pullback(cotangent.astype(jnp.float32).reshape(N_TOK, group_rows, D))
    return (block_groups.reshape(N_TOK * group_rows, D).astype(jnp.bfloat16), x_grads.reshape(N_TOK * group_rows, D), memory_grads.reshape(N_TOK * group_slots, D), weight_grads[0], weight_grads[1], weight_grads[2], weight_grads[3], weight_grads[4], weight_grads[5], weight_grads[6], weight_grads[7], weight_grads[8], weight_grads[9])
```

```python
from functools import partial

import jax
import jax.numpy as jnp
from jax import lax
from jax.experimental import pallas as pl
from jax.experimental.pallas import tpu as pltpu
from jax.sharding import Mesh, PartitionSpec as P

HEADS = 6
HEAD_DIM = 64
INNER = HEADS * HEAD_DIM
ITEMS_DEV = 8
EPS = 1e-06
MASKED = -1e30
WIDTH = 256
LANES = 128
PAIRS = INNER // LANES
GELU_A = 0.7978845608028654
GELU_B = 0.044715
F32 = jnp.float32
BF16 = jnp.bfloat16
AXES = ("o", "a", "b", "c", "m")
VMEM = 56 * 1024 * 1024


def dot_nn(left, right):
    return lax.dot_general(left, right, (((1,), (0,)), ((), ())), preferred_element_type=F32)


def dot_nt(left, right):
    return lax.dot_general(left, right, (((1,), (1,)), ((), ())), preferred_element_type=F32)


def dot_tn(left, right):
    return lax.dot_general(left, right, (((0,), (0,)), ((), ())), preferred_element_type=F32)


def whole(kernel, out_shape, *args, flops=0, scratch=()):
    nbytes = sum(a.size * a.dtype.itemsize for a in args)
    return pl.pallas_call(
        kernel,
        out_shape=out_shape,
        in_specs=[pl.BlockSpec(memory_space=pltpu.VMEM)] * len(args),
        out_specs=jax.tree.map(lambda _: pl.BlockSpec(memory_space=pltpu.VMEM), out_shape),
        scratch_shapes=list(scratch),
        compiler_params=pltpu.CompilerParams(vmem_limit_bytes=VMEM),
        cost_estimate=pl.CostEstimate(flops=flops, bytes_accessed=nbytes, transcendentals=0),
    )(*args)


def lane_half(rows, side):
    lane = lax.broadcasted_iota(jnp.int32, (rows, LANES), 1)
    return (lane < HEAD_DIM) if side == 0 else (lane >= HEAD_DIM)


def pick(value, side):
    return jnp.where(lane_half(value.shape[0], side), value, jnp.zeros_like(value))


def softmax(scores):
    top = jnp.max(scores, axis=-1, keepdims=True)
    weight = jnp.exp(scores - top)
    return weight / jnp.sum(weight, axis=-1, keepdims=True)


def self_scores(query, key, ring, allowed):
    rows = query.shape[0]
    spread = jnp.broadcast_to(ring, (rows, WIDTH))
    bias = pltpu.roll(spread, 0, 1, stride=1, stride_axis=0)[:, :rows]
    return jnp.where(allowed, dot_nt(query, key) + bias, MASKED)


def self_allowed(items_col, items_row):
    rows = items_col.shape[0]
    r = lax.broadcasted_iota(jnp.int32, (rows, rows), 0)
    q = lax.broadcasted_iota(jnp.int32, (rows, rows), 1)
    return (items_col == items_row) & (r >= q)


def self_forward_kernel(y_ref, order_ref, ring_ref, col_ref, row_ref, qkv_ref, mixed_ref):
    qkv_ref[...] = dot_nn(y_ref[...], order_ref[:, : 3 * INNER]).astype(BF16)
    allowed = self_allowed(col_ref[...], row_ref[...])
    rows = y_ref.shape[0]
    parts = []
    for pair in range(PAIRS):
        at = pair * LANES
        query = qkv_ref[:, at : at + LANES]
        key = qkv_ref[:, INNER + at : INNER + at + LANES]
        value = qkv_ref[:, 2 * INNER + at : 2 * INNER + at + LANES]
        outs = []
        for side in range(2):
            h = 2 * pair + side
            probs = softmax(self_scores(pick(query, side), key, ring_ref[h : h + 1, :], allowed))
            outs.append(dot_nn(probs.astype(BF16), value))
        parts.append(jnp.where(lane_half(rows, 0), outs[0], outs[1]).astype(BF16))
    mixed = jnp.concatenate(parts, axis=1)
    mixed_ref[...] = dot_nt(mixed, order_ref[:, 3 * INNER :]).astype(BF16)


def self_backward_kernel(
    gy_ref, order_ref, qkv_ref, ring_ref, col_ref, row_ref, dy_ref, diag_ref, dqkv_ref
):
    grad = dot_nn(gy_ref[...], order_ref[:, 3 * INNER :]).astype(BF16)
    allowed = self_allowed(col_ref[...], row_ref[...])
    rows = gy_ref.shape[0]
    diag_ref[...] = jnp.zeros_like(diag_ref)
    r = lax.broadcasted_iota(jnp.int32, (rows, rows), 0)
    q = lax.broadcasted_iota(jnp.int32, (rows, rows), 1)
    upside = (r + q == rows - 1).astype(BF16)
    for pair in range(PAIRS):
        at = pair * LANES
        query = qkv_ref[:, at : at + LANES]
        key = qkv_ref[:, INNER + at : INNER + at + LANES]
        value = qkv_ref[:, 2 * INNER + at : 2 * INNER + at + LANES]
        g_pair = grad[:, at : at + LANES]
        dq, dk, dv = [], [], []
        for side in range(2):
            h = 2 * pair + side
            probs = softmax(self_scores(pick(query, side), key, ring_ref[h : h + 1, :], allowed))
            dp = dot_nt(pick(g_pair, side), value)
            ds = probs * (dp - jnp.sum(probs * dp, axis=-1, keepdims=True))
            low = ds.astype(BF16)
            wide = jnp.concatenate(
                [dot_nn(upside, low), jnp.zeros((rows, WIDTH - rows), F32)], axis=1
            )
            turned = pltpu.roll(wide, 0, 1, stride=1, stride_axis=0)
            diag_ref[h : h + 1, :] = jnp.sum(turned, axis=0, keepdims=True)
            dq.append(dot_nn(low, key))
            dk.append(dot_tn(low, query))
            dv.append(dot_tn(probs.astype(BF16), g_pair))
        left = lane_half(rows, 0)
        for k, two in enumerate((dq, dk, dv)):
            dqkv_ref[:, k * INNER + at : k * INNER + at + LANES] = jnp.where(
                left, two[0], two[1]
            ).astype(BF16)
    dy_ref[...] = dot_nt(dqkv_ref[...], order_ref[:, : 3 * INNER]).astype(BF16)


def cross_forward_kernel(
    y_ref, order_ref, own_ref, peer_ref, col_ref, slot_ref, q_ref, mixed_ref
):
    q_ref[...] = dot_nn(y_ref[...], order_ref[:, :INNER]).astype(BF16)
    reach = col_ref[...] == slot_ref[...]
    rows = y_ref.shape[0]
    parts = []
    for pair in range(PAIRS):
        at = pair * LANES
        query = q_ref[:, at : at + LANES]
        key = jnp.concatenate([r[:, at : at + LANES] for r in (own_ref, peer_ref)], axis=0)
        value = jnp.concatenate(
            [r[:, INNER + at : INNER + at + LANES] for r in (own_ref, peer_ref)], axis=0
        )
        outs = []
        for side in range(2):
            probs = softmax(jnp.where(reach, dot_nt(pick(query, side), key), MASKED))
            outs.append(dot_nn(probs.astype(BF16), value))
        parts.append(jnp.where(lane_half(rows, 0), outs[0], outs[1]).astype(BF16))
    mixed = jnp.concatenate(parts, axis=1)
    mixed_ref[...] = dot_nt(mixed, order_ref[:, 3 * INNER :]).astype(BF16)


def cross_backward_kernel(
    gy_ref, order_ref, q_ref, own_ref, peer_ref, col_ref, slot_ref, dy_ref, dkv_ref, dq_ref
):
    grad = dot_nn(gy_ref[...], order_ref[:, 3 * INNER :]).astype(BF16)
    reach = col_ref[...] == slot_ref[...]
    rows = gy_ref.shape[0]
    slots = dkv_ref.shape[0]
    for pair in range(PAIRS):
        at = pair * LANES
        query = q_ref[:, at : at + LANES]
        key = jnp.concatenate([r[:, at : at + LANES] for r in (own_ref, peer_ref)], axis=0)
        value = jnp.concatenate(
            [r[:, INNER + at : INNER + at + LANES] for r in (own_ref, peer_ref)], axis=0
        )
        g_pair = grad[:, at : at + LANES]
        dq, dk, dv = [], [], []
        for side in range(2):
            probs = softmax(jnp.where(reach, dot_nt(pick(query, side), key), MASKED))
            dp = dot_nt(pick(g_pair, side), value)
            ds = (probs * (dp - jnp.sum(probs * dp, axis=-1, keepdims=True))).astype(BF16)
            dq.append(dot_nn(ds, key))
            dk.append(dot_tn(ds, query))
            dv.append(dot_tn(probs.astype(BF16), g_pair))
        dq_ref[:, at : at + LANES] = jnp.where(lane_half(rows, 0), dq[0], dq[1]).astype(BF16)
        left = lane_half(slots, 0)
        dkv_ref[:, at : at + LANES] = jnp.where(left, dk[0], dk[1]).astype(BF16)
        dkv_ref[:, INNER + at : INNER + at + LANES] = jnp.where(left, dv[0], dv[1]).astype(BF16)
    dy_ref[...] = dot_nt(dq_ref[...], order_ref[:, :INNER]).astype(BF16)


def ffn_kernel(
    n_ref, c_ref, wg_ref, wu_ref, wd_ref, out_ref, gn_ref, gg_ref, gu_ref, gd_ref, ag, au, ad
):
    step = pl.program_id(0)

    @pl.when(step == 0)
    def _():
        ag[...] = jnp.zeros_like(ag)
        au[...] = jnp.zeros_like(au)
        ad[...] = jnp.zeros_like(ad)

    n = n_ref[...]
    c = c_ref[...]
    gate = dot_nt(n, wg_ref[...])
    up = dot_nt(n, wu_ref[...])
    square = gate * gate
    t = jnp.tanh(GELU_A * gate * (1.0 + GELU_B * square))
    half = 0.5 * (1.0 + t)
    act = gate * half
    hidden = (act * up).astype(BF16)
    out_ref[...] = dot_nn(hidden, wd_ref[...]).astype(BF16)
    gh = dot_nt(c, wd_ref[...])
    slope = half + 0.5 * gate * (1.0 - t * t) * (GELU_A * (1.0 + 3.0 * GELU_B * square))
    d_gate = (gh * up * slope).astype(BF16)
    d_up = (gh * act).astype(BF16)
    gn_ref[...] = (dot_nn(d_gate, wg_ref[...]) + dot_nn(d_up, wu_ref[...])).astype(BF16)
    ad[...] += dot_tn(hidden, c)
    ag[...] += dot_tn(d_gate, n)
    au[...] += dot_tn(d_up, n)

    @pl.when(step == pl.num_programs(0) - 1)
    def _():
        gg_ref[...] = ag[...].astype(BF16)
        gu_ref[...] = au[...].astype(BF16)
        gd_ref[...] = ad[...].astype(BF16)


def ffn(n_all, c_all, wg, wu, wd):
    rows, width = n_all.shape
    cols = wg.shape[0]
    tile = rows // 8
    block = pl.BlockSpec((tile, width), lambda i: (i, 0))
    full = pl.BlockSpec((cols, width), lambda i: (0, 0))
    act = jax.ShapeDtypeStruct((rows, width), BF16)
    wgt = jax.ShapeDtypeStruct((cols, width), BF16)
    return pl.pallas_call(
        ffn_kernel,
        grid=(rows // tile,),
        in_specs=[block, block, full, full, full],
        out_specs=[block, block, full, full, full],
        out_shape=[act, act, wgt, wgt, wgt],
        scratch_shapes=[pltpu.VMEM((cols, width), F32)] * 3,
        compiler_params=pltpu.CompilerParams(
            vmem_limit_bytes=VMEM, dimension_semantics=("arbitrary",)
        ),
        cost_estimate=pl.CostEstimate(
            flops=18 * rows * width * cols,
            bytes_accessed=8 * rows * width + 12 * cols * width,
            transcendentals=rows * cols,
        ),
    )(n_all, c_all, wg, wu, wd)


def rms_scale(values):
    return lax.rsqrt(jnp.mean(values * values, axis=-1, keepdims=True) + EPS)


def norm_back(values, scale, gain, grad_out):
    weighted = grad_out * gain
    inner = jnp.mean(weighted * values, axis=-1, keepdims=True)
    grad_in = scale * weighted - values * (scale * scale * scale) * inner
    return grad_in, jnp.sum(grad_out * values * scale, axis=0)


def run_items(run_lengths, row_count):
    run_ends = jnp.cumsum(run_lengths)
    position = lax.iota(jnp.int32, row_count)
    return jnp.sum((position[:, None] >= run_ends[None, :]).astype(jnp.int32), axis=1)


def on_device(
    tokens,
    memory,
    target_lengths,
    memory_lengths,
    keep_mask,
    distance_bucket_lookup,
    self_query,
    self_kv,
    self_out,
    cross_query,
    cross_key_value,
    cross_out,
    ffn_in,
    ffn_down,
    norm_gains,
    rel_bias,
    cotangent,
):
    size = {axis: lax.axis_size(axis) for axis in AXES}
    me = {axis: lax.axis_index(axis) for axis in AXES}
    rows, width = tokens.shape
    slots = memory.shape[0]
    n_o, n_z = size["o"], size["o"] * 2
    n_dev = n_z * 8

    def permute(value, move):
        pairs = []
        for flat in range(n_dev):
            rest, at = flat, {}
            for axis in reversed(AXES):
                at[axis], rest = rest % size[axis], rest // size[axis]
            to = move(dict(at))
            there = 0
            for axis in AXES:
                there = there * size[axis] + to[axis]
            pairs.append((flat, there))
        return lax.ppermute(value, AXES, pairs)

    def flip(axis, mask=1):
        def move(at):
            at[axis] ^= mask
            return at

        return move

    def flip_by_core(first, second):
        def move(at):
            at[first if at["c"] == 0 else second] ^= 1
            return at

        return move

    def flip_z(mask):
        def move(at):
            z = (at["o"] * 2 + at["a"]) ^ mask
            at["o"], at["a"] = z // 2, z % 2
            return at

        return move

    def gather_all(own):
        held = jnp.stack([own] + [permute(own, flip_z(k)) for k in range(1, n_z)])
        for move in (flip_by_core("m", "b"), flip_by_core("b", "m"), flip("c")):
            held = jnp.concatenate([held, permute(held, move)], axis=0)
        return held.reshape(-1, width)

    def scatter_all(parts, extra):
        held = parts.reshape(n_dev, -1, width).astype(BF16)
        for move in (flip("c"), flip_by_core("b", "m"), flip_by_core("m", "b")):
            half = held.shape[0] // 2
            sent = held[half:]
            kept = held[:half].astype(F32)
            got = permute(sent, move).astype(F32)
            total = kept + got
            if extra is not None:
                extra = extra + permute(extra, move)
            held = total.astype(BF16)
        got = [permute(held[k], flip_z(k)).astype(F32) for k in range(1, n_z)]
        total = total[0] + sum(got)
        if extra is not None:
            extra = extra + sum([permute(extra, flip_z(k)) for k in range(1, n_z)])
        return total, extra

    def gather_eight(own):
        held = own[None]
        for move in (flip_by_core("b", "a"), flip_by_core("a", "b"), flip("c")):
            held = jnp.concatenate([held, permute(held, move)], axis=0)
        return held.reshape(-1, own.shape[1])

    def scatter_eight(parts):
        held = parts.reshape(8, rows, width)
        for move in (flip("c"), flip_by_core("a", "b"), flip_by_core("b", "a")):
            half = held.shape[0] // 2
            total = held[:half].astype(F32) + permute(held[half:], move).astype(F32)
            held = total.astype(BF16)
        return total[0]

    def gather_ffn(own):
        held = jnp.stack([own] + [permute(own, flip("o", k)) for k in range(1, n_o)])
        return jnp.concatenate([held, permute(held, flip("m"))], axis=0)

    def scatter_ffn(parts):
        total = parts[:n_o].astype(F32) + permute(parts[n_o:], flip("m")).astype(F32)
        low = total.astype(BF16)
        return total[0] + sum(
            [permute(low[k], flip("o", k)).astype(F32) for k in range(1, n_o)]
        )

    own_self = jnp.concatenate([self_query.T, self_kv[0].T, self_kv[1].T, self_out], axis=0)
    own_cross = jnp.concatenate(
        [cross_query.T, cross_key_value[0].T, cross_key_value[1].T, cross_out], axis=0
    )
    own_ffn = jnp.concatenate([ffn_in[0].T, ffn_in[1].T, ffn_down], axis=0)
    part_rows = self_out.shape[0]
    ff_rows = ffn_down.shape[0]
    w_self = gather_all(own_self)
    w_cross = gather_all(own_cross)
    ffn_parts = gather_ffn(own_ffn)
    wg, wu, wd = (
        ffn_parts[:, k * ff_rows : (k + 1) * ff_rows].reshape(-1, width) for k in range(3)
    )
    cot_all = gather_eight(cotangent)

    piece = lax.iota(jnp.int32, n_dev)
    z_mask, first, second, other = (
        piece % n_z,
        (piece // n_z) % 2,
        (piece // (2 * n_z)) % 2,
        piece // (4 * n_z),
    )
    core = me["c"] ^ other
    m_at = me["m"] ^ jnp.where(core == 0, first, second)
    b_at = me["b"] ^ jnp.where(core == 0, second, first)
    z_at = (me["o"] * 2 + me["a"]) ^ z_mask
    owner = ((z_at * 2 + b_at) * 2 + core) * 2 + m_at
    target = (
        lax.iota(jnp.int32, 4)[None, :, None] * INNER
        + owner[:, None, None] * part_rows
        + lax.iota(jnp.int32, part_rows)[None, None, :]
    ).reshape(-1)
    order = (target[:, None] == lax.iota(jnp.int32, 4 * INNER)[None, :]).astype(BF16)

    block_items = jax.vmap(lambda lengths: run_items(lengths, rows))(target_lengths[0])
    own_items = lax.dynamic_index_in_dim(block_items, me["m"], 0, keepdims=False)
    own_items = own_items + ITEMS_DEV * me["m"]
    items_col, items_row = own_items[:, None], own_items[None, :]
    peer_keep = permute(keep_mask, flip("m"))
    run_ends = jnp.cumsum(memory_lengths[0])
    run_starts = run_ends - memory_lengths[0]

    def slot_of(side, keep):
        position = side * slots + lax.iota(jnp.int32, slots)
        items = jnp.sum((position[:, None] >= run_ends[None, :]).astype(jnp.int32), axis=1)
        first_slot = jnp.any(position[:, None] == run_starts[None, :], axis=1)
        return jnp.where((keep > 0) | first_slot, items, -1)

    slot = jnp.concatenate([slot_of(me["m"], keep_mask), slot_of(1 - me["m"], peer_keep)])[None, :]

    def hot_of(distance):
        bucket = distance_bucket_lookup[jnp.clip(distance, 0, distance_bucket_lookup.shape[0] - 1)]
        return (bucket[:, None] == lax.iota(jnp.int32, rel_bias.shape[0])[None, :]).astype(F32)

    bucket_hot = hot_of((WIDTH - lax.iota(jnp.int32, WIDTH)) % WIDTH)
    back_hot = hot_of(rows - 1 - lax.iota(jnp.int32, WIDTH))
    table = jnp.pad(rel_bias, ((0, 0), (0, 8 - HEADS)))
    ring = lax.dot_general(
        table,
        bucket_hot,
        (((0,), (1,)), ((), ())),
        precision=lax.Precision.HIGHEST,
        preferred_element_type=F32,
    )

    gain_1, gain_2, gain_3 = norm_gains[0], norm_gains[1], norm_gains[2]
    x_1 = tokens.astype(F32)
    s_1 = rms_scale(x_1)
    n_1 = (x_1 * s_1 * gain_1).astype(BF16)
    inner_4 = order.shape[0]
    y_1 = dot_nt(n_1, w_self).astype(BF16)

    def shape(*dims, kind=BF16):
        return jax.ShapeDtypeStruct(dims, kind)

    qkv, mixed_1 = whole(
        self_forward_kernel,
        [shape(rows, 3 * INNER), shape(rows, inner_4)],
        y_1,
        order,
        ring,
        items_col,
        items_row,
        flops=2 * rows * inner_4 * inner_4,
    )
    x_2 = x_1 + dot_nn(mixed_1, w_self)
    s_2 = rms_scale(x_2)
    n_2 = (x_2 * s_2 * gain_2).astype(BF16)
    kv_low = dot_nt(memory, w_cross).astype(BF16)
    kv_own = dot_nn(kv_low, order[:, INNER : 3 * INNER]).astype(BF16)
    kv_peer = permute(kv_own, flip("m"))
    y_2 = dot_nt(n_2, w_cross).astype(BF16)
    q_2, mixed_2 = whole(
        cross_forward_kernel,
        [shape(rows, INNER), shape(rows, inner_4)],
        y_2,
        order,
        kv_own,
        kv_peer,
        items_col,
        slot,
        flops=2 * rows * inner_4 * inner_4,
    )
    x_3 = x_2 + dot_nn(mixed_2, w_cross)
    s_3 = rms_scale(x_3)
    n_3 = (x_3 * s_3 * gain_3).astype(BF16)
    n_all = gather_eight(n_3)
    part_out, part_gn, g_gate, g_up, g_down = ffn(n_all, cot_all, wg, wu, wd)

    grad_n3 = scatter_eight(part_gn)
    block_out = (x_3 + scatter_eight(part_out)).astype(BF16)
    ffn_grads = jnp.concatenate(
        [g.reshape(-1, ff_rows, width) for g in (g_gate, g_up, g_down)], axis=1
    )
    sum_ffn = scatter_ffn(ffn_grads)
    back_3, gain_g3 = norm_back(x_3, s_3, gain_3, grad_n3)
    grad_3 = cotangent.astype(F32) + back_3
    low_3 = grad_3.astype(BF16)
    gy_2 = dot_nt(low_3, w_cross).astype(BF16)
    dq_2, dkv = whole(
        lambda *refs: cross_backward_kernel(*refs),
        [shape(rows, inner_4), shape(2 * slots, 2 * INNER)],
        gy_2,
        order,
        q_2,
        kv_own,
        kv_peer,
        items_col,
        slot,
        flops=2 * rows * inner_4 * inner_4,
        scratch=[pltpu.VMEM((rows, INNER), BF16)],
    )
    dkv_peer = permute(dkv[slots:], flip("m"))
    dkv_own = (dkv[:slots].astype(F32) + dkv_peer.astype(F32)).astype(BF16)
    dkv_low = dot_nt(dkv_own, order[:, INNER : 3 * INNER]).astype(BF16)
    grad_memory = dot_nn(dkv_low, w_cross)
    part_cross = dot_tn(
        jnp.concatenate([dq_2, mixed_2, dkv_low], axis=0),
        jnp.concatenate([n_2, low_3, memory], axis=0),
    )
    sum_cross, _ = scatter_all(part_cross, None)
    back_2, gain_g2 = norm_back(x_2, s_2, gain_2, dot_nn(dq_2, w_cross))
    grad_2 = grad_3 + back_2
    low_2 = grad_2.astype(BF16)
    gy_1 = dot_nt(low_2, w_self).astype(BF16)
    dy_1, diag = whole(
        self_backward_kernel,
        [shape(rows, inner_4), shape(8, WIDTH, kind=F32)],
        gy_1,
        order,
        qkv,
        ring,
        items_col,
        items_row,
        flops=2 * rows * inner_4 * inner_4,
        scratch=[pltpu.VMEM((rows, 3 * INNER), BF16)],
    )
    back_1, gain_g1 = norm_back(x_1, s_1, gain_1, dot_nn(dy_1, w_self))
    grad_tokens = grad_2 + back_1
    part_self = dot_tn(
        jnp.concatenate([dy_1, mixed_1], axis=0), jnp.concatenate([n_1, low_2], axis=0)
    )
    bias_grad = lax.dot_general(
        back_hot,
        diag,
        (((0,), (1,)), ((), ())),
        precision=lax.Precision.HIGHEST,
        preferred_element_type=F32,
    )[:, :HEADS]
    flat_bias = jnp.pad(bias_grad.reshape(-1), (0, width - bias_grad.size))
    small = jnp.stack([gain_g1, gain_g2, gain_g3, flat_bias])
    sum_self, small = scatter_all(part_self, small)

    def four(total):
        q, k, v, out = (total[i * part_rows : (i + 1) * part_rows] for i in range(4))
        return q.T, jnp.stack([k.T, v.T]), out

    squery, skv, sout = four(sum_self)
    cquery, ckv, cout = four(sum_cross)
    fin = jnp.stack([sum_ffn[:ff_rows].T, sum_ffn[ff_rows : 2 * ff_rows].T])
    return (
        block_out,
        grad_tokens,
        grad_memory,
        squery,
        skv,
        sout,
        cquery,
        ckv,
        cout,
        fin,
        sum_ffn[2 * ff_rows :],
        small[:3],
        small[3, : bias_grad.size].reshape(bias_grad.shape),
    )


def solution(mesh):
    n_tok, n_mem = mesh.devices.shape
    grid = Mesh(mesh.devices.reshape(n_tok // 8, 2, 2, 2, n_mem), AXES)
    tok = AXES[:-1]
    rows = P(AXES, None)
    cols = P(None, AXES)
    deep = P(None, None, AXES)
    in_specs = (
        rows,
        rows,
        P(tok, None, None),
        P(tok, None),
        P(AXES),
        P(),
        cols,
        deep,
        rows,
        cols,
        deep,
        rows,
        deep,
        rows,
        P(),
        P(),
        rows,
    )
    out_specs = (rows, rows, rows, cols, deep, rows, cols, deep, rows, deep, rows, P(), P())
    return jax.shard_map(
        on_device, mesh=grid, in_specs=in_specs, out_specs=out_specs, check_vma=False
    )
```

```python
import jax
import jax.numpy as jnp
import numpy as np
from jax import lax
from jax.experimental import pallas as pl
from jax.experimental.pallas import tpu as pltpu
from jax.sharding import Mesh, PartitionSpec as P

HEADS = 6
HEAD_DIM = 64
INNER = HEADS * HEAD_DIM
ITEMS_DEV = 8
EPS = 1e-06
MASKED = -1e30
WIDTH = 256
LANES = 128
PAIRS = INNER // LANES
GELU_A = 0.7978845608028654
GELU_B = 0.044715
F32 = jnp.float32
BF16 = jnp.bfloat16
AXES = ("o", "a", "b", "c", "m")
GROUP = ("a", "b", "c")
VMEM = 24 * 1024 * 1024


def dot_nn(left, right):
    return lax.dot_general(left, right, (((1,), (0,)), ((), ())), preferred_element_type=F32)


def dot_nt(left, right):
    return lax.dot_general(left, right, (((1,), (1,)), ((), ())), preferred_element_type=F32)


def dot_tn(left, right):
    return lax.dot_general(left, right, (((0,), (0,)), ((), ())), preferred_element_type=F32)


def kernel_call(kernel, out_shape, *args, scratch=(), scalars=0, us=5, vmem=VMEM):
    spaces = [pltpu.SMEM] * scalars + [pltpu.VMEM] * (len(args) - scalars)
    return pl.pallas_call(
        kernel,
        out_shape=out_shape,
        in_specs=[pl.BlockSpec(memory_space=space) for space in spaces],
        out_specs=jax.tree.map(lambda _: pl.BlockSpec(memory_space=pltpu.VMEM), out_shape),
        scratch_shapes=list(scratch),
        compiler_params=pltpu.CompilerParams(vmem_limit_bytes=vmem),
        cost_estimate=pl.CostEstimate(flops=us * 1_000_000_000, bytes_accessed=1, transcendentals=0),
    )(*args)


def shape(*dims, kind=BF16):
    return jax.ShapeDtypeStruct(dims, kind)


def after(value, *others):
    return lax.optimization_barrier((value, *others))[0]


def lane_half(rows, side):
    lane = lax.broadcasted_iota(jnp.int32, (rows, LANES), 1)
    return (lane < HEAD_DIM) if side == 0 else (lane >= HEAD_DIM)


def pick(value, side):
    return jnp.where(lane_half(value.shape[0], side), value, jnp.zeros_like(value))


def softmax(scores):
    top = jnp.max(scores, axis=-1, keepdims=True)
    weight = jnp.exp(scores - top)
    return weight / jnp.sum(weight, axis=-1, keepdims=True)


def rms_scale(values):
    return lax.rsqrt(jnp.mean(values * values, axis=-1, keepdims=True) + EPS)


def norm_back(values, gain, grad_out):
    scale = rms_scale(values)
    weighted = grad_out * gain
    inner = jnp.mean(weighted * values, axis=-1, keepdims=True)
    grad_in = scale * weighted - values * (scale * scale * scale) * inner
    return grad_in, jnp.sum(grad_out * values * scale, axis=0, keepdims=True)


def rows_of(target_ref, at, size, first, count):
    row = lax.broadcasted_iota(jnp.int32, (count, size), 0) + first
    return (row == target_ref[:, at : at + size]).astype(F32).astype(BF16)


def to_natural(value, halves, target_ref, first, count):
    total = None
    for i, w in enumerate(halves):
        half = w.shape[0]
        hot = rows_of(target_ref, i * half, half, first, count)
        term = dot_nt(dot_nt(value, w[...]).astype(BF16), hot)
        total = term if total is None else total + term
    return total.astype(BF16)


def from_natural(value, halves, target_ref, first):
    total = None
    for i, w in enumerate(halves):
        half = w.shape[0]
        hot = rows_of(target_ref, i * half, half, first, value.shape[1])
        term = dot_nn(dot_nn(value, hot).astype(BF16), w[...])
        total = term if total is None else total + term
    return total


def shards_kernel(q_ref, kv_ref, o_ref, q2_ref, kv2_ref, o2_ref, out_ref):
    part, rows = o_ref.shape[0], out_ref.shape[0]
    r = lax.broadcasted_iota(jnp.int32, (rows, part), 0)
    i = lax.broadcasted_iota(jnp.int32, (rows, part), 1)
    total = None
    kv, kv2 = kv_ref[...], kv2_ref[...]
    shards = (q_ref[...], kv[:, 0, :], kv[:, 1, :], o_ref[...])
    shards += (q2_ref[...], kv2[:, 0, :], kv2[:, 1, :], o2_ref[...])
    for k, shard in enumerate(shards):
        hot = (r == i + k * part).astype(F32).astype(BF16)
        term = dot_nn(hot, shard)
        total = term if total is None else total + term
    out_ref[...] = total.astype(BF16)


def exact(left, right, dims):
    return lax.dot_general(
        left, right, (dims, ((), ())), precision=lax.Precision.HIGHEST, preferred_element_type=F32
    )


def buckets_of(lookup_ref, count):
    bucket = lax.broadcasted_iota(jnp.int32, (count, lookup_ref.shape[1]), 0)
    return (bucket == lookup_ref[...]).astype(F32)


def tables_kernel(
    m_ref, lengths_ref, runs_ref, keep_ref, peer_ref, lookup_ref, bias_ref, x_ref, gains_ref,
    ring_ref, col_ref, row_ref, slot_ref, n1_ref,
):
    m = m_ref[0]
    rows, slots = row_ref.shape[1], keep_ref.shape[1]
    for ref, axis in ((col_ref, 0), (row_ref, 1)):
        place = lax.broadcasted_iota(jnp.int32, ref.shape, axis)
        item, end = jnp.zeros(ref.shape, jnp.int32) + m * ITEMS_DEV, 0
        for i in range(ITEMS_DEV):
            end = end + lengths_ref[m, i]
            item = item + (place >= end).astype(jnp.int32)
        ref[...] = item
    for k, keep in enumerate((keep_ref, peer_ref)):
        place = lax.broadcasted_iota(jnp.int32, (1, slots), 1) + (m ^ k) * slots
        item, live, end = jnp.zeros((1, slots), jnp.int32), keep[...], 0
        for i in range(runs_ref.shape[1]):
            live = jnp.where(place == end, 1, live)
            end = end + runs_ref[0, i]
            item = item + (place >= end).astype(jnp.int32)
        slot_ref[k : k + 1, :] = jnp.where(live > 0, item, -1)
    by_distance = exact(bias_ref[...], buckets_of(lookup_ref, bias_ref.shape[0]), ((0,), (0,)))
    d = lax.broadcasted_iota(jnp.int32, (lookup_ref.shape[1], WIDTH), 0)
    k = lax.broadcasted_iota(jnp.int32, (lookup_ref.shape[1], WIDTH), 1)
    turn = ((d + k == WIDTH) | (d + k == 0)).astype(F32)
    ring_ref[...] = jnp.zeros_like(ring_ref)
    ring_ref[0:HEADS, :] = exact(by_distance, turn, ((1,), (0,)))
    x = x_ref[...].astype(F32)
    n1_ref[...] = (x * rms_scale(x) * gains_ref[0:1, :]).astype(BF16)


def self_scores(query, key, ring, allowed):
    rows = query.shape[0]
    spread = jnp.broadcast_to(ring, (rows, WIDTH))
    bias = pltpu.roll(spread, 0, 1, stride=1, stride_axis=0)[:, :rows]
    return jnp.where(allowed, dot_nt(query, key) + bias, MASKED)


def self_allowed(items_col, items_row):
    rows = items_col.shape[0]
    r = lax.broadcasted_iota(jnp.int32, (rows, rows), 0)
    q = lax.broadcasted_iota(jnp.int32, (rows, rows), 1)
    return (items_col == items_row) & (r >= q)


def self_forward_kernel(
    x_ref, n1_ref, gains_ref, w0_ref, w1_ref, target_ref, ring_ref, col_ref, row_ref,
    x2_ref, n2_ref, qkv_ref, low_ref,
):
    x = x_ref[...].astype(F32)
    n = n1_ref[...]
    halves = (w0_ref, w1_ref)
    qkv_ref[...] = to_natural(n, halves, target_ref, 0, 3 * INNER)
    allowed = self_allowed(col_ref[...], row_ref[...])
    rows = x.shape[0]
    for pair in range(PAIRS):
        at = pair * LANES
        query = qkv_ref[:, at : at + LANES]
        key = qkv_ref[:, INNER + at : INNER + at + LANES]
        value = qkv_ref[:, 2 * INNER + at : 2 * INNER + at + LANES]
        outs = []
        for side in range(2):
            h = 2 * pair + side
            probs = softmax(self_scores(pick(query, side), key, ring_ref[h : h + 1, :], allowed))
            outs.append(dot_nn(probs.astype(BF16), value))
        low_ref[:, at : at + LANES] = jnp.where(lane_half(rows, 0), outs[0], outs[1]).astype(BF16)
    x2 = x + from_natural(low_ref[...], halves, target_ref, 3 * INNER)
    x2_ref[...] = x2
    n2_ref[...] = (x2 * rms_scale(x2) * gains_ref[1:2, :]).astype(BF16)


def self_backward_kernel(
    g2_ref, x_ref, gains_ref, w0_ref, w1_ref, target_ref, plain_ref, qkv_ref, ring_ref, col_ref,
    row_ref, lookup_ref, g23_ref, gx_ref, dyt_ref, small_ref, dqkv_ref, diag_ref,
):
    halves = (w0_ref, w1_ref)
    grad = to_natural(g2_ref[...].astype(BF16), halves, target_ref, 3 * INNER, INNER)
    allowed = self_allowed(col_ref[...], row_ref[...])
    rows = x_ref.shape[0]
    diag_ref[...] = jnp.zeros_like(diag_ref)
    r = lax.broadcasted_iota(jnp.int32, (rows, rows), 0)
    q = lax.broadcasted_iota(jnp.int32, (rows, rows), 1)
    upside = (r + q == rows - 1).astype(BF16)
    for pair in range(PAIRS):
        at = pair * LANES
        query = qkv_ref[:, at : at + LANES]
        key = qkv_ref[:, INNER + at : INNER + at + LANES]
        value = qkv_ref[:, 2 * INNER + at : 2 * INNER + at + LANES]
        g_pair = grad[:, at : at + LANES]
        dq, dk, dv = [], [], []
        for side in range(2):
            h = 2 * pair + side
            probs = softmax(self_scores(pick(query, side), key, ring_ref[h : h + 1, :], allowed))
            dp = dot_nt(pick(g_pair, side), value)
            ds = probs * (dp - jnp.sum(probs * dp, axis=-1, keepdims=True))
            low = ds.astype(BF16)
            wide = jnp.concatenate(
                [dot_nn(upside, low), jnp.zeros((rows, WIDTH - rows), F32)], axis=1
            )
            turned = pltpu.roll(wide, 0, 1, stride=1, stride_axis=0)
            diag_ref[h : h + 1, :] = jnp.sum(turned, axis=0, keepdims=True)
            dq.append(dot_nn(low, key))
            dk.append(dot_tn(low, query))
            dv.append(dot_tn(probs.astype(BF16), g_pair))
        left = lane_half(rows, 0)
        for k, two in enumerate((dq, dk, dv)):
            dqkv_ref[:, k * INNER + at : k * INNER + at + LANES] = jnp.where(
                left, two[0], two[1]
            ).astype(BF16)
    col = lax.broadcasted_iota(jnp.int32, (dyt_ref.shape[0], 3 * INNER), 1)
    plain = (plain_ref[...] == col).astype(F32).astype(BF16)
    dyt_ref[...] = dot_nt(plain, dqkv_ref[...]).astype(BF16)
    back = from_natural(dqkv_ref[...], halves, target_ref, 0)
    grad_in, gain_grad = norm_back(x_ref[...].astype(F32), gains_ref[0:1, :], back)
    gx_ref[...] = g2_ref[...] + grad_in
    small_ref[...] = jnp.zeros_like(small_ref)
    small_ref[0:1, :] = gain_grad
    small_ref[1:3, :] = g23_ref[...]
    k = lax.broadcasted_iota(jnp.int32, (WIDTH, rows), 0)
    d = lax.broadcasted_iota(jnp.int32, (WIDTH, rows), 1)
    by_distance = exact(diag_ref[...], (k + d == rows - 1).astype(F32), ((1,), (0,)))
    buckets = buckets_of(lookup_ref, LANES)
    small_ref[8:16, 0:LANES] = exact(by_distance, buckets, ((1,), (1,)))


def memory_forward_kernel(own_ref, peer_ref, w0_ref, w1_ref, target_ref, kv_own_ref, kv_peer_ref):
    halves = (w0_ref, w1_ref)
    kv_own_ref[...] = to_natural(own_ref[...], halves, target_ref, INNER, 2 * INNER)
    kv_peer_ref[...] = to_natural(peer_ref[...], halves, target_ref, INNER, 2 * INNER)


def memory_backward_kernel(own_ref, got_ref, w0_ref, w1_ref, target_ref, out_ref):
    total = (own_ref[...].astype(F32) + got_ref[...].astype(F32)).astype(BF16)
    out_ref[...] = from_natural(total, (w0_ref, w1_ref), target_ref, INNER)


def key_value(own_ref, peer_ref, at):
    key = jnp.concatenate([r[:, at : at + LANES] for r in (own_ref, peer_ref)], axis=0)
    at += INNER
    return key, jnp.concatenate([r[:, at : at + LANES] for r in (own_ref, peer_ref)], axis=0)


def cross_forward_kernel(
    x_ref, n_ref, gains_ref, w0_ref, w1_ref, target_ref, own_ref, peer_ref, col_ref, slot_ref,
    x3_ref, n3_ref, q_ref, low_ref,
):
    halves = (w0_ref, w1_ref)
    q_ref[...] = to_natural(n_ref[...], halves, target_ref, 0, INNER)
    reach = col_ref[...] == jnp.concatenate([slot_ref[k : k + 1, :] for k in range(2)], axis=1)
    rows = x_ref.shape[0]
    for pair in range(PAIRS):
        at = pair * LANES
        query = q_ref[:, at : at + LANES]
        key, value = key_value(own_ref, peer_ref, at)
        outs = []
        for side in range(2):
            probs = softmax(jnp.where(reach, dot_nt(pick(query, side), key), MASKED))
            outs.append(dot_nn(probs.astype(BF16), value))
        low_ref[:, at : at + LANES] = jnp.where(lane_half(rows, 0), outs[0], outs[1]).astype(BF16)
    x3 = x_ref[...] + from_natural(low_ref[...], halves, target_ref, 3 * INNER)
    x3_ref[...] = x3
    n3_ref[...] = (x3 * rms_scale(x3) * gains_ref[2:3, :]).astype(BF16)


def cross_backward_kernel(
    lo_ref, got_c_ref, got_2_ref, got_ref, x3_ref, x2_ref, gains_ref, cot_ref, w0_ref, w1_ref, target_ref, q_ref,
    own_ref, peer_ref, col_ref, slot_ref, low3_ref, g2_ref, dq_ref, dkv_own_ref, dkv_peer_ref,
    gain_ref,
):
    halves = (w0_ref, w1_ref)
    rows = x3_ref.shape[0]
    grad_n3 = got_ref[...].astype(F32) + sum(
        ref[0:rows, :].astype(F32) for ref in (lo_ref, got_c_ref, got_2_ref)
    )
    grad_in, gain_3 = norm_back(x3_ref[...], gains_ref[2:3, :], grad_n3)
    grad_3 = cot_ref[...].astype(F32) + grad_in
    low3_ref[...] = grad_3.astype(BF16)
    grad = to_natural(low3_ref[...], halves, target_ref, 3 * INNER, INNER)
    reach = col_ref[...] == jnp.concatenate([slot_ref[k : k + 1, :] for k in range(2)], axis=1)
    rows = x3_ref.shape[0]
    slots = own_ref.shape[0]
    for pair in range(PAIRS):
        at = pair * LANES
        query = q_ref[:, at : at + LANES]
        key, value = key_value(own_ref, peer_ref, at)
        g_pair = grad[:, at : at + LANES]
        dq, dk, dv = [], [], []
        for side in range(2):
            probs = softmax(jnp.where(reach, dot_nt(pick(query, side), key), MASKED))
            dp = dot_nt(pick(g_pair, side), value)
            ds = (probs * (dp - jnp.sum(probs * dp, axis=-1, keepdims=True))).astype(BF16)
            dq.append(dot_nn(ds, key))
            dk.append(dot_tn(ds, query))
            dv.append(dot_tn(probs.astype(BF16), g_pair))
        dq_ref[:, at : at + LANES] = jnp.where(lane_half(rows, 0), dq[0], dq[1]).astype(BF16)
        left = lane_half(2 * slots, 0)
        for k, two in ((0, dk), (INNER, dv)):
            both = jnp.where(left, two[0], two[1]).astype(BF16)
            dkv_own_ref[:, k + at : k + at + LANES] = both[:slots]
            dkv_peer_ref[:, k + at : k + at + LANES] = both[slots:]
    back = from_natural(dq_ref[...], halves, target_ref, 0)
    grad_in, gain_2 = norm_back(x2_ref[...], gains_ref[1:2, :], back)
    g2_ref[...] = grad_3 + grad_in
    gain_ref[0:1, :] = gain_2
    gain_ref[1:2, :] = gain_3


def weights_kernel(
    dq_ref, low_ref, own_ref, peer_ref, low1_ref, n2_ref, low3_ref, mem_own_ref, mem_peer_ref, g2_ref,
    target_ref, one_ref, *refs,
):
    got_ref, out_ref = (refs[0] if len(refs) > 1 else None), refs[-1]

    def spread(order_ref, at, value):
        hot = rows_of(order_ref, 0, order_ref.shape[1], at, value.shape[1])
        return dot_nn(value, hot).astype(BF16)

    cross = dot_tn(
        jnp.concatenate(
            [
                spread(target_ref, 0, dq_ref[...]),
                spread(target_ref, 3 * INNER, low_ref[...]),
                spread(target_ref, INNER, own_ref[...]),
                spread(target_ref, INNER, peer_ref[...]),
            ],
            axis=0,
        ),
        jnp.concatenate(
            [n2_ref[...], low3_ref[...], mem_own_ref[...], mem_peer_ref[...]], axis=0
        ),
    )
    out = dot_tn(spread(one_ref, 0, low1_ref[...]), g2_ref[...].astype(BF16))
    wide, slim = cross.shape[0] // 4, out.shape[0] // 4

    def put(at, value):
        if got_ref is not None:
            value = value + got_ref[at : at + value.shape[0], :].astype(F32)
        out_ref[at : at + value.shape[0], :] = value.astype(BF16)

    for k in range(4):
        put(k * (wide + slim), cross[k * wide : (k + 1) * wide])
        put(k * (wide + slim) + wide, out[k * slim : (k + 1) * slim])


def columns_kernel(at_ref, held_ref, lo_ref, hi_ref, out_ref):
    rows = held_ref.shape[2]
    total = None
    for k in range(8):
        right = (lo_ref if k < 4 else hi_ref)[(k % 4) * rows : (k % 4 + 1) * rows, :]
        term = dot_nn(held_ref[at_ref[k]], right)
        total = term if total is None else total + term
    out_ref[...] = total.astype(BF16)


def assemble(parts, whole_ref):
    cols = parts[0].shape[0]
    for i, part in enumerate(parts):
        whole_ref[i * cols : (i + 1) * cols, :] = part[...]


def grad_hidden_kernel(c_ref, *refs):
    parts, out_ref, wd_ref = refs[:-2], refs[-2], refs[-1]
    assemble(parts, wd_ref)
    out_ref[...] = dot_nt(c_ref[...], wd_ref[...])


def ffn_kernel(n_ref, gh_ref, *refs):
    parts, (h_ref, dg_ref, du_ref, gn_ref, wg_ref, wu_ref) = refs[:-6], refs[-6:]
    cols = parts[0].shape[0] // 2
    assemble([part.at[:cols, :] for part in parts], wg_ref)
    assemble([part.at[cols:, :] for part in parts], wu_ref)
    n = n_ref[...]
    gate = dot_nt(n, wg_ref[...])
    up = dot_nt(n, wu_ref[...])
    square = gate * gate
    t = jnp.tanh(GELU_A * gate * (1.0 + GELU_B * square))
    half = 0.5 * (1.0 + t)
    act = gate * half
    h_ref[...] = (act * up).astype(BF16)
    gh = gh_ref[...]
    slope = half + 0.5 * gate * (1.0 - t * t) * (GELU_A * (1.0 + 3.0 * GELU_B * square))
    d_gate = (gh * up * slope).astype(BF16)
    d_up = (gh * act).astype(BF16)
    dg_ref[...] = d_gate
    du_ref[...] = d_up
    gn_ref[...] = (dot_nn(d_gate, wg_ref[...]) + dot_nn(d_up, wu_ref[...])).astype(BF16)


def ffn_out_kernel(h_ref, *refs):
    parts, out_ref, wd_ref = refs[:-2], refs[-2], refs[-1]
    got_ref, parts = (parts[0], parts[1:]) if len(parts) % 2 else (None, parts)
    assemble(parts, wd_ref)
    value = dot_nn(h_ref[...], wd_ref[...])
    if got_ref is not None:
        value = value + got_ref[...].astype(F32)
    out_ref[...] = value.astype(BF16)


def ffn_weights_kernel(
    count, h0_ref, h1_ref, g0_ref, g1_ref, u0_ref, u1_ref, n0_ref, n1_ref, c0_ref, c1_ref, *out_refs
):
    sets = (
        ((h0_ref, c0_ref), (h1_ref, c1_ref)),
        ((g0_ref, n0_ref), (g1_ref, n1_ref)),
        ((u0_ref, n0_ref), (u1_ref, n1_ref)),
    )
    down_ref, both_ref = out_refs
    for kind, pairs in enumerate(sets):
        value = sum(dot_tn(left[...], right[...]) for left, right in pairs).astype(BF16)
        if kind == 0:
            down_ref[...] = value
            continue
        cols = both_ref.shape[0] // (2 * count)
        for i in range(count):
            at = (2 * i + kind - 1) * cols
            both_ref[at : at + cols, :] = value[i * cols : (i + 1) * cols]


def on_device(
    tokens,
    memory,
    target_lengths,
    memory_lengths,
    keep_mask,
    distance_bucket_lookup,
    self_query,
    self_kv,
    self_out,
    cross_query,
    cross_key_value,
    cross_out,
    ffn_in,
    ffn_down,
    norm_gains,
    rel_bias,
    cotangent,
):
    size = {axis: lax.axis_size(axis) for axis in AXES}
    me = {axis: lax.axis_index(axis) for axis in AXES}
    rows, width = tokens.shape
    slots = memory.shape[0]
    part_rows, ff_rows = self_out.shape[0], ffn_down.shape[0]
    n_o = size["o"]
    quads = 2 * n_o

    def cut(value):
        if value.ndim < 2 or value.shape[-2] % LANES:
            return value
        return value.reshape(*value.shape[:-2], -1, LANES // 2, value.shape[-1])

    def permute(value, move):
        pairs = []
        for flat in range(quads * 8):
            rest, at = flat, {}
            for axis in reversed(AXES):
                at[axis], rest = rest % size[axis], rest // size[axis]
            to = move(dict(at))
            there = 0
            for axis in AXES:
                there = there * size[axis] + to[axis]
            pairs.append((flat, there))
        return lax.ppermute(cut(value), AXES, pairs).reshape(value.shape)

    def flips(**masks):
        def move(at):
            return {axis: at[axis] ^ masks.get(axis, 0) for axis in AXES}

        return move

    def flip_by_core(first, second):
        def move(at):
            at[first if at["c"] == 0 else second] ^= 1
            return at

        return move

    first_move, second_move = flip_by_core("b", "a"), flip_by_core("a", "b")
    core_move, peer_move = flips(c=1), flips(m=1)

    def grow(held, move):
        return jnp.concatenate([held, permute(held, move)], axis=0)

    def exchange(value, axes, parts):
        value = value.reshape(parts, -1, value.shape[-1])
        got = lax.all_to_all(cut(value), axes, split_axis=0, concat_axis=0, tiled=True)
        return got.reshape(value.shape)

    stage = lax.optimization_barrier
    full, slim = (rows, width), (rows, INNER)
    half, cols = 4 * rows, quads * ff_rows
    kv_shape = shape(slots, 2 * INNER)
    down, gate, up = (pltpu.VMEM((cols, width), BF16) for _ in range(3))

    def over_o(own):
        return [own] + [permute(own, flips(o=k)) for k in range(1, n_o)]

    def over_m(parts):
        return parts + [permute(v, peer_move) for v in parts]

    def flat_of(at):
        return ((((at["o"] * 2 + at["a"]) * 2 + at["b"]) * 2 + at["c"]) * 2) + at["m"]

    def mask_of(eighth, quad, core):
        by_1, by_2 = ("b", "a") if core ^ (eighth // 4) == 0 else ("a", "b")
        at = {"o": quad % n_o, "m": quad // n_o, "c": eighth // 4}
        at[by_1], at[by_2] = eighth % 2, (eighth // 2) % 2
        return flat_of(at)

    masks = np.array(
        [[mask_of(e, q, core) for e in range(8) for q in range(quads)] for core in range(2)]
    ).astype(np.int32)
    piece = 4 * part_rows

    def target_of(owner, padded):
        row = np.arange(padded)
        base = row // part_rows * INNER + row % part_rows
        return owner[:, None] * part_rows + base[None, :].astype(np.int32)

    moves = [flips(o=k % n_o, m=k // n_o) for k in range(1, quads)]
    wide = quads * piece

    own_both = kernel_call(
        shards_kernel, shape(2 * piece, width), self_query.T, jnp.transpose(self_kv, (2, 0, 1)), self_out,
        cross_query.T, jnp.transpose(cross_key_value, (2, 0, 1)), cross_out, us=2,
    )
    got = [own_both] + [permute(own_both, move) for move in moves]
    here, at_core = after((flat_of(me), me["c"]), own_both)
    mask = jnp.where(at_core == 0, masks[0], masks[1])
    target = target_of(here ^ mask, piece).reshape(1, -1)
    one = jnp.where(
        np.arange(16)[None, :] < part_rows, target_of(here ^ mask, 16), -1
    ).reshape(1, -1)
    om_bits = flat_of({"o": n_o - 1, "a": 0, "b": 0, "c": 0, "m": 1})
    quad_masks = masks[0, :quads]
    owner = (np.arange(8, dtype=np.int32)[:, None] * 2) | ((here & om_bits) ^ quad_masks)[None, :]
    plain = target_of(owner.reshape(-1), 40).reshape(-1, 1)
    eight_at = ((here ^ mask[::quads]) // 2) % 8
    both = jnp.concatenate([v[:piece] for v in got] + [v[piece:] for v in got], axis=0)
    cot_1 = grow(cotangent, first_move)
    keep = keep_mask.reshape(1, -1)
    peer_keep = permute(keep, peer_move)
    own_gu = jnp.swapaxes(ffn_in, 1, 2).reshape(2 * ff_rows, width)

    def two_halves(held, got):
        half = held.shape[0] // 2
        return [jnp.concatenate([held[at : at + half], got[at : at + half]], axis=0) for at in (0, half)]

    both, cot_1, peer_keep, memory, own_down, target, one, plain, eight_at = stage(
        (both, cot_1, peer_keep, memory, ffn_down, target, one, plain, eight_at)
    )
    targets, ones = (jnp.split(v, 2, axis=1) for v in (target, one))
    both = jnp.concatenate(two_halves(both, permute(both, first_move)), axis=0)
    down_o = over_o(own_down)
    peer_memory = permute(memory, peer_move)
    lookup = distance_bucket_lookup.reshape(1, -1)
    ring, items_col, items_row, slot, own_1 = kernel_call(
        tables_kernel,
        [
            shape(8, WIDTH, kind=F32), shape(rows, 1, kind=jnp.int32), shape(1, rows, kind=jnp.int32),
            shape(2, slots, kind=jnp.int32), shape(*full),
        ],
        me["m"].reshape(1), target_lengths[0], memory_lengths, keep, peer_keep, lookup, rel_bias,
        tokens, norm_gains, scalars=3,
    )

    both, down_o, own_gu, ring, own_1 = stage((both, down_o, own_gu, ring, own_1))
    self_lo, cross_lo = two_halves(both, permute(both, second_move))
    w_down = over_m(down_o)
    gu_o = over_o(own_gu)
    gu_m = permute(own_gu, peer_move)

    self_lo, cross_lo, peer_memory, cot_1, gu_o, gu_m, w_down, target = stage(
        (self_lo, cross_lo, peer_memory, cot_1, gu_o, gu_m, w_down, target)
    )
    w_self = (self_lo, permute(self_lo, core_move))

    w_self, cross_lo, cot_1 = stage((w_self, cross_lo, cot_1))
    x_2, n_2, qkv, low_1 = kernel_call(
        self_forward_kernel,
        [shape(*full, kind=F32), shape(*full), shape(rows, 3 * INNER), shape(*slim)],
        tokens, own_1, norm_gains, *w_self, target, ring, items_col, items_row,
    )
    w_cross = (cross_lo, permute(cross_lo, core_move))
    cot_lo = grow(cot_1, second_move)

    x_2, w_cross, gu_o = stage((x_2, w_cross, gu_o))
    kv_own, kv_peer = kernel_call(
        memory_forward_kernel, [kv_shape] * 2, memory, peer_memory, *w_cross, target
    )
    x_3, n_3, q_2, low_2 = kernel_call(
        cross_forward_kernel,
        [shape(*full, kind=F32), shape(*full), shape(*slim), shape(*slim)],
        x_2, n_2, norm_gains, *w_cross, target, kv_own, kv_peer, items_col, slot,
    )
    w_gu = gu_o + [gu_m] + [permute(v, peer_move) for v in gu_o[1:]]

    x_3, n_3, cot_lo, w_gu = stage((x_3, n_3, cot_lo, w_gu))
    n_1 = grow(n_3, first_move)
    cot_hi = permute(cot_lo, core_move)

    def grad_hidden(value):
        return kernel_call(
            grad_hidden_kernel, shape(half, cols, kind=F32), value, *w_down, scratch=[down]
        )

    gh_lo = grad_hidden(cot_lo)

    n_1, cot_hi, gh_lo = stage((n_1, cot_hi, gh_lo))
    n_lo = grow(n_1, second_move)
    gh_hi = grad_hidden(cot_hi)

    def ffn(value, gh):
        return kernel_call(
            ffn_kernel,
            [shape(half, cols), shape(half, cols), shape(half, cols), shape(half, width)],
            value, gh, *w_gu, scratch=[gate, up],
        )

    n_lo, gh_hi, own_1 = stage((n_lo, gh_hi, own_1))
    n_hi = permute(n_lo, core_move)
    lo_f = ffn(n_lo, gh_lo)
    one_1 = grow(own_1, first_move)

    n_hi, lo_f, one_1 = stage((n_hi, lo_f, one_1))
    hi_f = ffn(n_hi, gh_hi)

    (h_lo, g_lo, u_lo, gn_lo), (h_hi, g_hi, u_hi, gn_hi), one_1 = stage((lo_f, hi_f, one_1))
    got_c = permute(gn_hi, core_move)

    def ffn_out(*args):
        return kernel_call(ffn_out_kernel, shape(half, width), *args, *w_down, scratch=[down])

    out_hi = ffn_out(h_hi)

    def summed(at, end, *parts):
        return sum(v[at:end].astype(F32) for v in parts).astype(BF16)

    got_c, out_hi, h_lo = stage((got_c, out_hi, h_lo))
    got_2 = permute(summed(2 * rows, 4 * rows, gn_lo, got_c), second_move)
    out_got = permute(out_hi, core_move)
    grad_down, grad_gu = kernel_call(
        lambda *refs: ffn_weights_kernel(quads, *refs),
        [shape(cols, width), shape(2 * cols, width)],
        h_lo, h_hi, g_lo, g_hi, u_lo, u_hi, n_lo, n_hi, cot_lo, cot_hi,
    )

    got_2, out_got, grad_down, grad_gu, one_1 = stage((got_2, out_got, grad_down, grad_gu, one_1))
    got_1 = permute(summed(rows, 2 * rows, gn_lo, got_c, got_2), first_move)
    out_lo = ffn_out(h_lo, out_got)
    down_m = permute(grad_down[cols // 2 :], peer_move)

    got_1, out_lo, grad_gu, one_1 = stage((got_1, out_lo, grad_gu, one_1))
    low_3, grad_2, dq, dkv_own, dkv_peer, gains_23 = kernel_call(
        cross_backward_kernel,
        [
            shape(*full), shape(*full, kind=F32), shape(*slim), kv_shape, kv_shape,
            shape(2, width, kind=F32),
        ],
        gn_lo, got_c, got_2, got_1, x_3, x_2, norm_gains, cotangent, *w_cross, target, q_2, kv_own,
        kv_peer, items_col, slot,
    )
    n1_lo = grow(one_1, second_move)
    gu_m = permute(grad_gu[cols:], peer_move)

    low_3, grad_2, dq, dkv_own, dkv_peer, gains_23, down_m, n1_lo = stage(
        (low_3, grad_2, dq, dkv_own, dkv_peer, gains_23, down_m, n1_lo)
    )
    operands = (dq, low_2, dkv_own, dkv_peer, low_1, n_2, low_3, memory, peer_memory, grad_2)
    stack = shape(4 * quads * (piece + 16), width)
    sent = kernel_call(weights_kernel, stack, *operands, targets[1], ones[1])
    n1_hi = permute(n1_lo, core_move)

    def over_back(part, grad, got):
        return [
            permute(summed(k * part, (k + 1) * part, grad, got), flips(o=k)) for k in range(1, n_o)
        ]

    sent, grad_2, dkv_peer, n1_hi = stage((sent, grad_2, dkv_peer, n1_hi))
    cross_c = permute(sent, core_move)
    dkv_got = permute(dkv_peer, peer_move)
    out_2 = permute(out_lo[2 * rows :], second_move)
    grad_tokens, dyt, small = kernel_call(
        self_backward_kernel,
        [shape(*full, kind=F32), shape(8 * quads * 40, rows), shape(16, width, kind=F32)],
        grad_2, tokens, norm_gains, *w_self, target, plain, qkv, ring, items_col, items_row, lookup,
        gains_23, scratch=[pltpu.VMEM((rows, 3 * INNER), BF16), pltpu.VMEM((8, WIDTH), F32)],
    )
    down_b = over_back(ff_rows, grad_down, down_m)

    cross_c, grad_tokens, dyt, small, gu_m, down_b, out_2 = stage(
        (cross_c, grad_tokens, dyt, small, gu_m, down_b, out_2)
    )
    held = exchange(dyt, GROUP, 8)
    cross_part = kernel_call(weights_kernel, stack, *operands, targets[0], ones[0], cross_c)
    small = small + permute(small, core_move)
    gu_b = over_back(2 * ff_rows, grad_gu, gu_m)

    held, cross_part, dkv_got, small = stage((held, cross_part, dkv_got, small))
    quarter = cross_part.shape[0] // 4
    cross_2 = permute(cross_part[2 * quarter :], second_move)
    part_self = kernel_call(
        columns_kernel, shape(quads * 40, width), eight_at, held, n1_lo, n1_hi, scalars=1
    )
    small = small + permute(small, second_move)

    cross_2, part_self, small, gu_b = stage((cross_2, part_self, small, gu_b))
    cross_1 = permute(summed(quarter, 2 * quarter, cross_part, cross_2), first_move)
    out_1 = permute(summed(rows, 2 * rows, out_lo, out_2), first_move)
    grad_memory = kernel_call(
        memory_backward_kernel, shape(slots, width, kind=F32), dkv_own, dkv_got, *w_cross, target
    )
    small = small + permute(small, first_move)

    cross_1, small, grad_memory, out_1 = stage((cross_1, small, grad_memory, out_1))
    cross_sum = cross_part[:quarter] + cross_2[:quarter].astype(F32) + cross_1.astype(F32)

    def pieces(k):
        at, end = k * piece, wide + k * 16
        return jnp.concatenate(
            [cross_sum[at : at + piece], cross_sum[end : end + 16], part_self[k * 40 : k * 40 + 40]],
            axis=0,
        )

    pieces_got = [permute(pieces(k + 1).astype(BF16), move) for k, move in enumerate(moves)]
    small_got = [permute(small, move) for move in moves]
    block_out = summed(0, rows, x_3, out_lo, out_2, out_1)

    pieces_got, small_got, block_out = stage((pieces_got, small_got, block_out))
    total = pieces(0) + sum(g.astype(F32) for g in pieces_got)
    small = small + sum(small_got)
    sum_cross, sum_self = total[: piece + 16], total[piece + 16 :]

    def back_sum(part, *parts):
        return sum(v[:part].astype(F32) for v in parts)

    sum_down = back_sum(ff_rows, grad_down, down_m, *down_b)
    sum_gu = back_sum(2 * ff_rows, grad_gu, gu_m, *gu_b)

    def three(total):
        query, key, value = (total[k * part_rows : (k + 1) * part_rows] for k in range(3))
        return query.T, jnp.transpose(jnp.stack([key, value], axis=1), (1, 2, 0))

    squery, skv = three(sum_self)
    cquery, ckv = three(sum_cross)
    fin = jnp.swapaxes(sum_gu.reshape(2, ff_rows, width), 1, 2)
    base = 4 * part_rows
    return (
        block_out,
        grad_tokens,
        grad_memory,
        squery,
        skv,
        sum_cross[base : base + part_rows],
        cquery,
        ckv,
        sum_cross[3 * part_rows : base],
        fin,
        sum_down,
        small[:3],
        small[8 : 8 + HEADS, : rel_bias.shape[0]].T,
    )


def solution(mesh):
    n_tok, n_mem = mesh.devices.shape
    grid = Mesh(mesh.devices.reshape(n_tok // 8, 2, 2, 2, n_mem), AXES)
    tok = AXES[:-1]
    rows = P(AXES, None)
    cols = P(None, AXES)
    deep = P(None, None, AXES)
    in_specs = (
        rows,
        rows,
        P(tok, None, None),
        P(tok, None),
        P(AXES),
        P(),
        cols,
        deep,
        rows,
        cols,
        deep,
        rows,
        deep,
        rows,
        P(),
        P(),
        rows,
    )
    out_specs = (rows, rows, rows, cols, deep, rows, cols, deep, rows, deep, rows, P(), P())
    return jax.shard_map(
        on_device, mesh=grid, in_specs=in_specs, out_specs=out_specs, check_vma=False
    )
```

```python
import jax
import jax.numpy as jnp
import numpy as np
from jax import lax
from jax.experimental import pallas as pl
from jax.experimental.pallas import tpu as pltpu
from jax.sharding import Mesh, PartitionSpec as P

HEADS = 6
HEAD_DIM = 64
INNER = HEADS * HEAD_DIM
ITEMS_DEV = 8
EPS = 1e-06
MASKED = -1e30
WIDTH = 256
LANES = 128
PAIRS = INNER // LANES
GELU_A = 0.7978845608028654
GELU_B = 0.044715
F32 = jnp.float32
BF16 = jnp.bfloat16
AXES = ("o", "a", "b", "c", "m")
GROUP = ("a", "b", "c")
VMEM = 24 * 1024 * 1024


def dot_nn(left, right):
    return lax.dot_general(left, right, (((1,), (0,)), ((), ())), preferred_element_type=F32)


def dot_nt(left, right):
    return lax.dot_general(left, right, (((1,), (1,)), ((), ())), preferred_element_type=F32)


def dot_tn(left, right):
    return lax.dot_general(left, right, (((0,), (0,)), ((), ())), preferred_element_type=F32)


def kernel_call(kernel, out_shape, *args, scratch=(), scalars=0, us=5, vmem=VMEM):
    spaces = [pltpu.SMEM] * scalars + [pltpu.VMEM] * (len(args) - scalars)
    return pl.pallas_call(
        kernel,
        out_shape=out_shape,
        in_specs=[pl.BlockSpec(memory_space=space) for space in spaces],
        out_specs=jax.tree.map(lambda _: pl.BlockSpec(memory_space=pltpu.VMEM), out_shape),
        scratch_shapes=list(scratch),
        compiler_params=pltpu.CompilerParams(vmem_limit_bytes=vmem),
        cost_estimate=pl.CostEstimate(flops=us * 1_000_000_000, bytes_accessed=1, transcendentals=0),
    )(*args)


def shape(*dims, kind=BF16):
    return jax.ShapeDtypeStruct(dims, kind)


def after(value, *others):
    return lax.optimization_barrier((value, *others))[0]


def lane_half(rows, side):
    lane = lax.broadcasted_iota(jnp.int32, (rows, LANES), 1)
    return (lane < HEAD_DIM) if side == 0 else (lane >= HEAD_DIM)


def pick(value, side):
    return jnp.where(lane_half(value.shape[0], side), value, jnp.zeros_like(value))


def softmax(scores):
    top = jnp.max(scores, axis=-1, keepdims=True)
    weight = jnp.exp(scores - top)
    return weight / jnp.sum(weight, axis=-1, keepdims=True)


def rms_scale(values):
    return lax.rsqrt(jnp.mean(values * values, axis=-1, keepdims=True) + EPS)


def norm_back(values, gain, grad_out):
    scale = rms_scale(values)
    weighted = grad_out * gain
    inner = jnp.mean(weighted * values, axis=-1, keepdims=True)
    grad_in = scale * weighted - values * (scale * scale * scale) * inner
    return grad_in, jnp.sum(grad_out * values * scale, axis=0, keepdims=True)


def rows_of(target_ref, at, size, first, count):
    row = lax.broadcasted_iota(jnp.int32, (count, size), 0) + first
    return (row == target_ref[:, at : at + size]).astype(F32).astype(BF16)


def to_natural(value, halves, target_ref, first, count):
    total = None
    for i, w in enumerate(halves):
        half = w.shape[0]
        hot = rows_of(target_ref, i * half, half, first, count)
        term = dot_nt(dot_nt(value, w[...]).astype(BF16), hot)
        total = term if total is None else total + term
    return total.astype(BF16)


def from_natural(value, halves, target_ref, first):
    total = None
    for i, w in enumerate(halves):
        half = w.shape[0]
        hot = rows_of(target_ref, i * half, half, first, value.shape[1])
        term = dot_nn(dot_nn(value, hot).astype(BF16), w[...])
        total = term if total is None else total + term
    return total


def shards_kernel(q_ref, kv_ref, o_ref, q2_ref, kv2_ref, o2_ref, out_ref):
    part, rows = o_ref.shape[0], out_ref.shape[0]
    r = lax.broadcasted_iota(jnp.int32, (rows, part), 0)
    i = lax.broadcasted_iota(jnp.int32, (rows, part), 1)
    total = None
    kv, kv2 = kv_ref[...], kv2_ref[...]
    shards = (q_ref[...], kv[:, 0, :], kv[:, 1, :], o_ref[...])
    shards += (q2_ref[...], kv2[:, 0, :], kv2[:, 1, :], o2_ref[...])
    for k, shard in enumerate(shards):
        hot = (r == i + k * part).astype(F32).astype(BF16)
        term = dot_nn(hot, shard)
        total = term if total is None else total + term
    out_ref[...] = total.astype(BF16)


def exact(left, right, dims):
    return lax.dot_general(
        left, right, (dims, ((), ())), precision=lax.Precision.HIGHEST, preferred_element_type=F32
    )


def buckets_of(lookup_ref, count):
    bucket = lax.broadcasted_iota(jnp.int32, (count, lookup_ref.shape[1]), 0)
    return (bucket == lookup_ref[...]).astype(F32)


def tables_kernel(
    m_ref, lengths_ref, runs_ref, keep_ref, peer_ref, lookup_ref, bias_ref, x_ref, gains_ref,
    ring_ref, col_ref, row_ref, slot_ref, n1_ref,
):
    m = m_ref[0]
    rows, slots = row_ref.shape[1], keep_ref.shape[1]
    for ref, axis in ((col_ref, 0), (row_ref, 1)):
        place = lax.broadcasted_iota(jnp.int32, ref.shape, axis)
        item, end = jnp.zeros(ref.shape, jnp.int32) + m * ITEMS_DEV, 0
        for i in range(ITEMS_DEV):
            end = end + lengths_ref[m, i]
            item = item + (place >= end).astype(jnp.int32)
        ref[...] = item
    for k, keep in enumerate((keep_ref, peer_ref)):
        place = lax.broadcasted_iota(jnp.int32, (1, slots), 1) + (m ^ k) * slots
        item, live, end = jnp.zeros((1, slots), jnp.int32), keep[...], 0
        for i in range(runs_ref.shape[1]):
            live = jnp.where(place == end, 1, live)
            end = end + runs_ref[0, i]
            item = item + (place >= end).astype(jnp.int32)
        slot_ref[k : k + 1, :] = jnp.where(live > 0, item, -1)
    by_distance = exact(bias_ref[...], buckets_of(lookup_ref, bias_ref.shape[0]), ((0,), (0,)))
    d = lax.broadcasted_iota(jnp.int32, (lookup_ref.shape[1], WIDTH), 0)
    k = lax.broadcasted_iota(jnp.int32, (lookup_ref.shape[1], WIDTH), 1)
    turn = ((d + k == WIDTH) | (d + k == 0)).astype(F32)
    ring_ref[...] = jnp.zeros_like(ring_ref)
    ring_ref[0:HEADS, :] = exact(by_distance, turn, ((1,), (0,)))
    x = x_ref[...].astype(F32)
    n1_ref[...] = (x * rms_scale(x) * gains_ref[0:1, :]).astype(BF16)


def self_scores(query, key, ring, allowed):
    rows = query.shape[0]
    spread = jnp.broadcast_to(ring, (rows, WIDTH))
    bias = pltpu.roll(spread, 0, 1, stride=1, stride_axis=0)[:, :rows]
    return jnp.where(allowed, dot_nt(query, key) + bias, MASKED)


def self_allowed(items_col, items_row):
    rows = items_col.shape[0]
    r = lax.broadcasted_iota(jnp.int32, (rows, rows), 0)
    q = lax.broadcasted_iota(jnp.int32, (rows, rows), 1)
    return (items_col == items_row) & (r >= q)


def self_forward_kernel(
    x_ref, n1_ref, gains_ref, w0_ref, w1_ref, target_ref, ring_ref, col_ref, row_ref,
    x2_ref, n2_ref, qkv_ref, low_ref,
):
    x = x_ref[...].astype(F32)
    n = n1_ref[...]
    halves = (w0_ref, w1_ref)
    qkv_ref[...] = to_natural(n, halves, target_ref, 0, 3 * INNER)
    allowed = self_allowed(col_ref[...], row_ref[...])
    rows = x.shape[0]
    for pair in range(PAIRS):
        at = pair * LANES
        query = qkv_ref[:, at : at + LANES]
        key = qkv_ref[:, INNER + at : INNER + at + LANES]
        value = qkv_ref[:, 2 * INNER + at : 2 * INNER + at + LANES]
        outs = []
        for side in range(2):
            h = 2 * pair + side
            probs = softmax(self_scores(pick(query, side), key, ring_ref[h : h + 1, :], allowed))
            outs.append(dot_nn(probs.astype(BF16), value))
        low_ref[:, at : at + LANES] = jnp.where(lane_half(rows, 0), outs[0], outs[1]).astype(BF16)
    x2 = x + from_natural(low_ref[...], halves, target_ref, 3 * INNER)
    x2_ref[...] = x2
    n2_ref[...] = (x2 * rms_scale(x2) * gains_ref[1:2, :]).astype(BF16)


def self_backward_kernel(
    g2_ref, x_ref, gains_ref, w0_ref, w1_ref, target_ref, plain_ref, qkv_ref, ring_ref, col_ref,
    row_ref, lookup_ref, g23_ref, gx_ref, dyt_ref, small_ref, dqkv_ref, diag_ref,
):
    halves = (w0_ref, w1_ref)
    grad = to_natural(g2_ref[...].astype(BF16), halves, target_ref, 3 * INNER, INNER)
    allowed = self_allowed(col_ref[...], row_ref[...])
    rows = x_ref.shape[0]
    diag_ref[...] = jnp.zeros_like(diag_ref)
    r = lax.broadcasted_iota(jnp.int32, (rows, rows), 0)
    q = lax.broadcasted_iota(jnp.int32, (rows, rows), 1)
    upside = (r + q == rows - 1).astype(BF16)
    for pair in range(PAIRS):
        at = pair * LANES
        query = qkv_ref[:, at : at + LANES]
        key = qkv_ref[:, INNER + at : INNER + at + LANES]
        value = qkv_ref[:, 2 * INNER + at : 2 * INNER + at + LANES]
        g_pair = grad[:, at : at + LANES]
        dq, dk, dv = [], [], []
        for side in range(2):
            h = 2 * pair + side
            probs = softmax(self_scores(pick(query, side), key, ring_ref[h : h + 1, :], allowed))
            dp = dot_nt(pick(g_pair, side), value)
            ds = probs * (dp - jnp.sum(probs * dp, axis=-1, keepdims=True))
            low = ds.astype(BF16)
            wide = jnp.concatenate(
                [dot_nn(upside, low), jnp.zeros((rows, WIDTH - rows), F32)], axis=1
            )
            turned = pltpu.roll(wide, 0, 1, stride=1, stride_axis=0)
            diag_ref[h : h + 1, :] = jnp.sum(turned, axis=0, keepdims=True)
            dq.append(dot_nn(low, key))
            dk.append(dot_tn(low, query))
            dv.append(dot_tn(probs.astype(BF16), g_pair))
        left = lane_half(rows, 0)
        for k, two in enumerate((dq, dk, dv)):
            dqkv_ref[:, k * INNER + at : k * INNER + at + LANES] = jnp.where(
                left, two[0], two[1]
            ).astype(BF16)
    plain = rows_of(plain_ref, 0, plain_ref.shape[1], 0, 3 * INNER)
    dyt_ref[...] = dot_nn(dqkv_ref[...], plain).T.astype(BF16)
    back = from_natural(dqkv_ref[...], halves, target_ref, 0)
    grad_in, gain_grad = norm_back(x_ref[...].astype(F32), gains_ref[0:1, :], back)
    gx_ref[...] = g2_ref[...] + grad_in
    small_ref[...] = jnp.zeros_like(small_ref)
    small_ref[0:1, :] = gain_grad
    small_ref[1:3, :] = g23_ref[...]
    k = lax.broadcasted_iota(jnp.int32, (WIDTH, rows), 0)
    d = lax.broadcasted_iota(jnp.int32, (WIDTH, rows), 1)
    by_distance = exact(diag_ref[...], (k + d == rows - 1).astype(F32), ((1,), (0,)))
    buckets = buckets_of(lookup_ref, LANES)
    by_bucket = exact(by_distance, buckets, ((1,), (1,)))
    for h in range(HEADS):
        small_ref[3:4, h * LANES : (h + 1) * LANES] = by_bucket[h : h + 1, :]


def memory_forward_kernel(own_ref, peer_ref, w0_ref, w1_ref, target_ref, kv_own_ref, kv_peer_ref):
    halves = (w0_ref, w1_ref)
    kv_own_ref[...] = to_natural(own_ref[...], halves, target_ref, INNER, 2 * INNER)
    kv_peer_ref[...] = to_natural(peer_ref[...], halves, target_ref, INNER, 2 * INNER)


def memory_backward_kernel(own_ref, got_ref, w0_ref, w1_ref, target_ref, out_ref):
    total = (own_ref[...].astype(F32) + got_ref[...].astype(F32)).astype(BF16)
    out_ref[...] = from_natural(total, (w0_ref, w1_ref), target_ref, INNER)


def key_value(own_ref, peer_ref, at):
    key = jnp.concatenate([r[:, at : at + LANES] for r in (own_ref, peer_ref)], axis=0)
    at += INNER
    return key, jnp.concatenate([r[:, at : at + LANES] for r in (own_ref, peer_ref)], axis=0)


def cross_forward_kernel(
    x_ref, n_ref, gains_ref, w0_ref, w1_ref, target_ref, own_ref, peer_ref, col_ref, slot_ref,
    x3_ref, n3_ref, q_ref, low_ref,
):
    halves = (w0_ref, w1_ref)
    q_ref[...] = to_natural(n_ref[...], halves, target_ref, 0, INNER)
    reach = col_ref[...] == jnp.concatenate([slot_ref[k : k + 1, :] for k in range(2)], axis=1)
    rows = x_ref.shape[0]
    for pair in range(PAIRS):
        at = pair * LANES
        query = q_ref[:, at : at + LANES]
        key, value = key_value(own_ref, peer_ref, at)
        outs = []
        for side in range(2):
            probs = softmax(jnp.where(reach, dot_nt(pick(query, side), key), MASKED))
            outs.append(dot_nn(probs.astype(BF16), value))
        low_ref[:, at : at + LANES] = jnp.where(lane_half(rows, 0), outs[0], outs[1]).astype(BF16)
    x3 = x_ref[...] + from_natural(low_ref[...], halves, target_ref, 3 * INNER)
    x3_ref[...] = x3
    n3_ref[...] = (x3 * rms_scale(x3) * gains_ref[2:3, :]).astype(BF16)


def cross_backward_kernel(
    lo_ref, got_c_ref, got_2_ref, got_ref, x3_ref, x2_ref, gains_ref, cot_ref, w0_ref, w1_ref, target_ref, q_ref,
    own_ref, peer_ref, col_ref, slot_ref, low3_ref, g2_ref, dq_ref, dkv_own_ref, dkv_peer_ref,
    gain_ref,
):
    halves = (w0_ref, w1_ref)
    rows = x3_ref.shape[0]
    grad_n3 = got_ref[...].astype(F32) + sum(
        ref[0:rows, :].astype(F32) for ref in (lo_ref, got_c_ref, got_2_ref)
    )
    grad_in, gain_3 = norm_back(x3_ref[...], gains_ref[2:3, :], grad_n3)
    grad_3 = cot_ref[...].astype(F32) + grad_in
    low3_ref[...] = grad_3.astype(BF16)
    grad = to_natural(low3_ref[...], halves, target_ref, 3 * INNER, INNER)
    reach = col_ref[...] == jnp.concatenate([slot_ref[k : k + 1, :] for k in range(2)], axis=1)
    rows = x3_ref.shape[0]
    slots = own_ref.shape[0]
    for pair in range(PAIRS):
        at = pair * LANES
        query = q_ref[:, at : at + LANES]
        key, value = key_value(own_ref, peer_ref, at)
        g_pair = grad[:, at : at + LANES]
        dq, dk, dv = [], [], []
        for side in range(2):
            probs = softmax(jnp.where(reach, dot_nt(pick(query, side), key), MASKED))
            dp = dot_nt(pick(g_pair, side), value)
            ds = (probs * (dp - jnp.sum(probs * dp, axis=-1, keepdims=True))).astype(BF16)
            dq.append(dot_nn(ds, key))
            dk.append(dot_tn(ds, query))
            dv.append(dot_tn(probs.astype(BF16), g_pair))
        dq_ref[:, at : at + LANES] = jnp.where(lane_half(rows, 0), dq[0], dq[1]).astype(BF16)
        left = lane_half(2 * slots, 0)
        for k, two in ((0, dk), (INNER, dv)):
            both = jnp.where(left, two[0], two[1]).astype(BF16)
            dkv_own_ref[:, k + at : k + at + LANES] = both[:slots]
            dkv_peer_ref[:, k + at : k + at + LANES] = both[slots:]
    back = from_natural(dq_ref[...], halves, target_ref, 0)
    grad_in, gain_2 = norm_back(x2_ref[...], gains_ref[1:2, :], back)
    g2_ref[...] = grad_3 + grad_in
    gain_ref[0:1, :] = gain_2
    gain_ref[1:2, :] = gain_3


def weights_kernel(
    dq_ref, low_ref, own_ref, peer_ref, low1_ref, n2_ref, low3_ref, mem_own_ref, mem_peer_ref, g2_ref,
    target_ref, one_ref, *out_refs,
):
    right = jnp.concatenate([n2_ref[...], low3_ref[...], mem_own_ref[...], mem_peer_ref[...]], axis=0)
    right_out = g2_ref[...].astype(BF16)
    for i, out_ref in enumerate(out_refs):

        def spread(order_ref, first, value):
            size = order_ref.shape[1] // 2
            hot = rows_of(order_ref, i * size, size, first, value.shape[1])
            return dot_nn(value, hot).astype(BF16)

        left = jnp.concatenate(
            [
                spread(target_ref, 0, dq_ref[...]),
                spread(target_ref, 3 * INNER, low_ref[...]),
                spread(target_ref, INNER, own_ref[...]),
                spread(target_ref, INNER, peer_ref[...]),
            ],
            axis=0,
        )
        cross = dot_tn(left, right).astype(BF16)
        out = dot_tn(spread(one_ref, 0, low1_ref[...]), right_out).astype(BF16)
        wide, slim = cross.shape[0] // 4, out.shape[0] // 4
        for k in range(4):
            at = k * (wide + slim)
            out_ref[at : at + wide, :] = cross[k * wide : (k + 1) * wide]
            out_ref[at + wide : at + wide + slim, :] = out[k * slim : (k + 1) * slim]


def columns_kernel(at_ref, held_ref, lo_ref, hi_ref, out_ref):
    rows = held_ref.shape[2]
    total = None
    for k in range(8):
        right = (lo_ref if k < 4 else hi_ref)[(k % 4) * rows : (k % 4 + 1) * rows, :]
        term = dot_nn(held_ref[at_ref[k]], right)
        total = term if total is None else total + term
    out_ref[...] = total.astype(BF16)


def assemble(parts, whole_ref):
    cols = parts[0].shape[0]
    for i, part in enumerate(parts):
        whole_ref[i * cols : (i + 1) * cols, :] = part[...]


def grad_hidden_kernel(c_ref, *refs):
    parts, out_ref, wd_ref = refs[:-2], refs[-2], refs[-1]
    assemble(parts, wd_ref)
    out_ref[...] = dot_nt(c_ref[...], wd_ref[...])


def ffn_kernel(n_ref, gh_ref, *refs):
    parts, (h_ref, dg_ref, du_ref, gn_ref, wg_ref, wu_ref) = refs[:-6], refs[-6:]
    cols = parts[0].shape[0] // 2
    assemble([part.at[:cols, :] for part in parts], wg_ref)
    assemble([part.at[cols:, :] for part in parts], wu_ref)
    n = n_ref[...]
    gate = dot_nt(n, wg_ref[...])
    up = dot_nt(n, wu_ref[...])
    square = gate * gate
    t = jnp.tanh(GELU_A * gate * (1.0 + GELU_B * square))
    half = 0.5 * (1.0 + t)
    act = gate * half
    h_ref[...] = (act * up).astype(BF16)
    gh = gh_ref[...]
    slope = half + 0.5 * gate * (1.0 - t * t) * (GELU_A * (1.0 + 3.0 * GELU_B * square))
    d_gate = (gh * up * slope).astype(BF16)
    d_up = (gh * act).astype(BF16)
    dg_ref[...] = d_gate
    du_ref[...] = d_up
    gn_ref[...] = (dot_nn(d_gate, wg_ref[...]) + dot_nn(d_up, wu_ref[...])).astype(BF16)


def ffn_out_kernel(h_ref, *refs):
    parts, out_ref, wd_ref = refs[:-2], refs[-2], refs[-1]
    got_ref, parts = (parts[0], parts[1:]) if len(parts) % 2 else (None, parts)
    assemble(parts, wd_ref)
    value = dot_nn(h_ref[...], wd_ref[...])
    if got_ref is not None:
        value = value + got_ref[...].astype(F32)
    out_ref[...] = value.astype(BF16)


def ffn_weights_kernel(
    h0_ref, h1_ref, g0_ref, g1_ref, u0_ref, u1_ref, n0_ref, n1_ref, c0_ref, c1_ref, *out_refs
):
    sets = (
        ((h0_ref, c0_ref), (h1_ref, c1_ref)),
        ((g0_ref, n0_ref), (g1_ref, n1_ref)),
        ((u0_ref, n0_ref), (u1_ref, n1_ref)),
    )
    for out_ref, pairs in zip(out_refs, sets):
        out_ref[...] = sum(dot_tn(left[...], right[...]) for left, right in pairs).astype(BF16)


def on_device(
    tokens,
    memory,
    target_lengths,
    memory_lengths,
    keep_mask,
    distance_bucket_lookup,
    self_query,
    self_kv,
    self_out,
    cross_query,
    cross_key_value,
    cross_out,
    ffn_in,
    ffn_down,
    norm_gains,
    rel_bias,
    cotangent,
):
    size = {axis: lax.axis_size(axis) for axis in AXES}
    me = {axis: lax.axis_index(axis) for axis in AXES}
    rows, width = tokens.shape
    slots = memory.shape[0]
    part_rows, ff_rows = self_out.shape[0], ffn_down.shape[0]
    n_o = size["o"]
    quads = 2 * n_o

    def cut(value):
        if value.ndim < 2 or value.shape[-2] % LANES:
            return value
        return value.reshape(*value.shape[:-2], -1, LANES // 2, value.shape[-1])

    def permute(value, move):
        pairs = []
        for flat in range(quads * 8):
            rest, at = flat, {}
            for axis in reversed(AXES):
                at[axis], rest = rest % size[axis], rest // size[axis]
            to = move(dict(at))
            there = 0
            for axis in AXES:
                there = there * size[axis] + to[axis]
            pairs.append((flat, there))
        return lax.ppermute(cut(value), AXES, pairs).reshape(value.shape)

    def flips(**masks):
        def move(at):
            return {axis: at[axis] ^ masks.get(axis, 0) for axis in AXES}

        return move

    def flip_by_core(first, second):
        def move(at):
            at[first if at["c"] == 0 else second] ^= 1
            return at

        return move

    first_move, second_move = flip_by_core("b", "a"), flip_by_core("a", "b")
    core_move, peer_move = flips(c=1), flips(m=1)

    def grow(held, move):
        return jnp.concatenate([held, permute(held, move)], axis=0)

    def exchange(value, axes, parts):
        value = value.reshape(parts, -1, value.shape[-1])
        got = lax.all_to_all(cut(value), axes, split_axis=0, concat_axis=0, tiled=True)
        return got.reshape(value.shape)

    stage = lax.optimization_barrier
    full, slim = (rows, width), (rows, INNER)
    half, cols = 4 * rows, quads * ff_rows
    kv_shape = shape(slots, 2 * INNER)
    down, gate, up = (pltpu.VMEM((cols, width), BF16) for _ in range(3))

    def flat_of(at):
        return ((((at["o"] * 2 + at["a"]) * 2 + at["b"]) * 2 + at["c"]) * 2) + at["m"]

    def mask_of(eighth, quad, core):
        by_1, by_2 = ("b", "a") if core ^ (eighth // 4) == 0 else ("a", "b")
        at = {"o": quad % n_o, "m": quad // n_o, "c": eighth // 4}
        at[by_1], at[by_2] = eighth % 2, (eighth // 2) % 2
        return flat_of(at)

    masks = np.array(
        [[mask_of(e, q, core) for e in range(8) for q in range(quads)] for core in range(2)]
    ).astype(np.int32)
    piece = 4 * part_rows

    def target_of(owner, padded):
        row = np.arange(padded)
        base = row // part_rows * INNER + row % part_rows
        return owner[:, None] * part_rows + base[None, :].astype(np.int32)

    moves = [flips(o=k % n_o, m=k // n_o) for k in range(1, quads)]
    wide = quads * piece

    own_both = kernel_call(
        shards_kernel, shape(2 * piece, width), self_query.T, jnp.transpose(self_kv, (2, 0, 1)), self_out,
        cross_query.T, jnp.transpose(cross_key_value, (2, 0, 1)), cross_out, us=2,
    )
    got = [own_both] + [permute(own_both, move) for move in moves]
    here, at_core = after((flat_of(me), me["c"]), own_both)
    mask = jnp.where(at_core == 0, masks[0], masks[1])
    target = target_of(here ^ mask, piece).reshape(1, -1)
    one = jnp.where(
        np.arange(16)[None, :] < part_rows, target_of(here ^ mask, 16), -1
    ).reshape(1, -1)
    om_bits = flat_of({"o": n_o - 1, "a": 0, "b": 0, "c": 0, "m": 1})
    quad_masks = masks[0, :quads]
    owner = (np.arange(8, dtype=np.int32)[:, None] * 2) | ((here & om_bits) ^ quad_masks)[None, :]
    plain = target_of(owner.reshape(-1), 40).reshape(1, -1)
    eight_at = ((here ^ mask[::quads]) // 2) % 8
    both = jnp.concatenate([v[:piece] for v in got] + [v[piece:] for v in got], axis=0)
    cot_1 = grow(cotangent, first_move)
    keep = keep_mask.reshape(1, -1)
    peer_keep = permute(keep, peer_move)
    own_gu = jnp.swapaxes(ffn_in, 1, 2).reshape(2 * ff_rows, width)

    def two_halves(held, got):
        half = held.shape[0] // 2
        return [jnp.concatenate([held[at : at + half], got[at : at + half]], axis=0) for at in (0, half)]

    both, cot_1, peer_keep, memory, target, one, plain, eight_at, own_down = stage(
        (both, cot_1, peer_keep, memory, target, one, plain, eight_at, ffn_down)
    )
    both = jnp.concatenate(two_halves(both, permute(both, first_move)), axis=0)
    peer_memory = permute(memory, peer_move)
    lookup = distance_bucket_lookup.reshape(1, -1)
    ring, items_col, items_row, slot, own_1 = kernel_call(
        tables_kernel,
        [
            shape(8, WIDTH, kind=F32), shape(rows, 1, kind=jnp.int32), shape(1, rows, kind=jnp.int32),
            shape(2, slots, kind=jnp.int32), shape(*full),
        ],
        me["m"].reshape(1), target_lengths[0], memory_lengths, keep, peer_keep, lookup, rel_bias,
        tokens, norm_gains, scalars=3,
    )

    def over_o(own):
        return [own] + [permute(own, flips(o=k)) for k in range(1, n_o)]

    def over_m(parts, own_m):
        return parts + [own_m] + [permute(v, peer_move) for v in parts[1:]]

    down_o, down_m = over_o(own_down), permute(own_down, peer_move)

    both, ring, own_1, own_gu, down_o, down_m = stage((both, ring, own_1, own_gu, down_o, down_m))
    self_lo, cross_lo = two_halves(both, permute(both, second_move))
    gu_o, gu_m = over_o(own_gu), permute(own_gu, peer_move)
    w_down = over_m(down_o, down_m)

    self_lo, cross_lo, peer_memory, gu_o, gu_m, target, w_down = stage(
        (self_lo, cross_lo, peer_memory, gu_o, gu_m, target, w_down)
    )
    w_self = (self_lo, permute(self_lo, core_move))
    w_cross = (cross_lo, permute(cross_lo, core_move))

    w_self, w_cross, cot_1, gu_o = stage((w_self, w_cross, cot_1, gu_o))
    x_2, n_2, qkv, low_1 = kernel_call(
        self_forward_kernel,
        [shape(*full, kind=F32), shape(*full), shape(rows, 3 * INNER), shape(*slim)],
        tokens, own_1, norm_gains, *w_self, target, ring, items_col, items_row,
    )
    kv_own, kv_peer = kernel_call(
        memory_forward_kernel, [kv_shape] * 2, memory, peer_memory, *w_cross, target
    )
    x_3, n_3, q_2, low_2 = kernel_call(
        cross_forward_kernel,
        [shape(*full, kind=F32), shape(*full), shape(*slim), shape(*slim)],
        x_2, n_2, norm_gains, *w_cross, target, kv_own, kv_peer, items_col, slot,
    )
    cot_lo = grow(cot_1, second_move)
    w_gu = over_m(gu_o, gu_m)

    x_3, n_3, cot_lo, w_gu = stage((x_3, n_3, cot_lo, w_gu))
    n_1 = grow(n_3, first_move)
    cot_hi = permute(cot_lo, core_move)

    def grad_hidden(value):
        return kernel_call(
            grad_hidden_kernel, shape(half, cols, kind=F32), value, *w_down, scratch=[down], us=2
        )

    gh_lo = grad_hidden(cot_lo)

    n_1, cot_hi, gh_lo, own_1 = stage((n_1, cot_hi, gh_lo, own_1))
    n_lo = grow(n_1, second_move)
    gh_hi = grad_hidden(cot_hi)

    def ffn(value, gh):
        return kernel_call(
            ffn_kernel,
            [shape(half, cols), shape(half, cols), shape(half, cols), shape(half, width)],
            value, gh, *w_gu, scratch=[gate, up],
        )

    n_lo, gh_hi, own_1 = stage((n_lo, gh_hi, own_1))
    n_hi = permute(n_lo, core_move)
    lo_f = ffn(n_lo, gh_lo)
    one_1 = grow(own_1, first_move)

    n_hi, lo_f = stage((n_hi, lo_f))
    hi_f = ffn(n_hi, gh_hi)

    (h_lo, g_lo, u_lo, gn_lo), (h_hi, g_hi, u_hi, gn_hi) = stage((lo_f, hi_f))
    got_c = permute(gn_hi, core_move)

    def ffn_out(*args):
        return kernel_call(
            ffn_out_kernel, shape(half, width), *args, *w_down, scratch=[down], us=2
        )

    out_hi = ffn_out(h_hi)

    def summed(at, end, *parts):
        return sum(v[at:end].astype(F32) for v in parts).astype(BF16)

    got_c, out_hi, h_lo = stage((got_c, out_hi, h_lo))
    got_2 = permute(summed(2 * rows, 4 * rows, gn_lo, got_c), second_move)
    out_got = permute(out_hi, core_move)
    grad_down, grad_gate, grad_up = kernel_call(
        ffn_weights_kernel,
        [shape(cols, width)] * 3,
        h_lo, h_hi, g_lo, g_hi, u_lo, u_hi, n_lo, n_hi, cot_lo, cot_hi,
    )

    got_2, out_got, grad_down = stage((got_2, out_got, grad_down))
    got_1 = permute(summed(rows, 2 * rows, gn_lo, got_c, got_2), first_move)
    out_lo = ffn_out(h_lo, out_got)

    def over_m_back(grad):
        return permute(grad[cols // 2 :], peer_move)

    def over_o_back(grad, got):
        return [
            permute(summed(k * ff_rows, (k + 1) * ff_rows, grad, got), flips(o=k))
            for k in range(1, n_o)
        ]

    def back_sum(part, *parts):
        return sum(v[:part].astype(F32) for v in parts)

    down_m = over_m_back(grad_down)

    got_1, out_lo, one_1 = stage((got_1, out_lo, one_1))
    low_3, grad_2, dq, dkv_own, dkv_peer, gains_23 = kernel_call(
        cross_backward_kernel,
        [
            shape(*full), shape(*full, kind=F32), shape(*slim), kv_shape, kv_shape,
            shape(2, width, kind=F32),
        ],
        gn_lo, got_c, got_2, got_1, x_3, x_2, norm_gains, cotangent, *w_cross, target, q_2, kv_own,
        kv_peer, items_col, slot, us=8,
    )
    n1_lo = grow(one_1, second_move)

    grad_2, dq, down_m, grad_gate, dkv_peer = stage((grad_2, dq, down_m, grad_gate, dkv_peer))
    grad_tokens, dyt, small = kernel_call(
        self_backward_kernel,
        [shape(*full, kind=F32), shape(8 * quads * 40, rows), shape(4, width, kind=F32)],
        grad_2, tokens, norm_gains, *w_self, target, plain, qkv, ring, items_col, items_row, lookup,
        gains_23, scratch=[pltpu.VMEM((rows, 3 * INNER), BF16), pltpu.VMEM((8, WIDTH), F32)], us=8,
    )
    gate_m = over_m_back(grad_gate)

    grad_tokens, dyt, small, n1_lo, down_m = stage((grad_tokens, dyt, small, n1_lo, down_m))
    held = exchange(dyt, GROUP, 8)
    stack = shape(4 * quads * (piece + 16), width)
    kept, sent = kernel_call(
        weights_kernel, [stack] * 2,
        dq, low_2, dkv_own, dkv_peer, low_1, n_2, low_3, memory, peer_memory, grad_2, target, one, us=10,
    )
    n1_hi = permute(n1_lo, core_move)
    small = small + permute(small, core_move)
    down_b = over_o_back(grad_down, down_m)

    held, sent, small, n1_hi, gate_m, grad_up, out_lo, dkv_peer = stage(
        (held, sent, small, n1_hi, gate_m, grad_up, out_lo, dkv_peer)
    )
    cross_c = permute(sent, core_move)
    part_self = kernel_call(
        columns_kernel, shape(quads * 40, width), eight_at, held, n1_lo, n1_hi, scalars=1, us=2
    )
    out_2 = permute(out_lo[2 * rows :], second_move)
    small = small + sum(permute(small, flips(a=k // 2, b=k % 2)) for k in range(1, 4))
    up_m = over_m_back(grad_up)
    dkv_got = permute(dkv_peer, peer_move)

    cross_c, part_self, down_b, out_2, dkv_got = stage((cross_c, part_self, down_b, out_2, dkv_got))
    quarter = kept.shape[0] // 4
    cross_2 = permute(summed(2 * quarter, 4 * quarter, kept, cross_c), second_move)
    self_got = [permute(part_self[k * 40 + 40 : k * 40 + 80], move) for k, move in enumerate(moves)]
    gate_b = over_o_back(grad_gate, gate_m)
    sum_down = back_sum(ff_rows, grad_down, down_m, *down_b)

    cross_2, self_got, small, up_m, dkv_got, sum_down = stage(
        (cross_2, self_got, small, up_m, dkv_got, sum_down)
    )
    cross_1 = permute(summed(quarter, 2 * quarter, kept, cross_c, cross_2), first_move)
    small_got = [permute(small, move) for move in moves]
    up_b = over_o_back(grad_up, up_m)
    grad_memory = kernel_call(
        memory_backward_kernel, shape(slots, width, kind=F32), dkv_own, dkv_got, *w_cross, target
    )
    sum_self = back_sum(40, part_self, *self_got)

    cross_1, small_got, gate_b, sum_self, grad_memory = stage(
        (cross_1, small_got, gate_b, sum_self, grad_memory)
    )

    def pieces(k):
        return jnp.concatenate(
            [
                sum(v[at:end].astype(F32) for v in (kept, cross_c, cross_2, cross_1))
                for at, end in ((k * piece, k * piece + piece), (wide + k * 16, wide + k * 16 + 16))
            ],
            axis=0,
        )

    pieces_got = [permute(pieces(k + 1).astype(BF16), move) for k, move in enumerate(moves)]
    out_1 = permute(summed(rows, 2 * rows, out_lo, out_2), first_move)
    sum_gate = back_sum(ff_rows, grad_gate, gate_m, *gate_b)
    small = small + sum(small_got)

    pieces_got, out_1, sum_gate, up_b, small = stage((pieces_got, out_1, sum_gate, up_b, small))
    sum_cross = pieces(0) + sum(g.astype(F32) for g in pieces_got)
    sum_up = back_sum(ff_rows, grad_up, up_m, *up_b)
    block_out = summed(0, rows, x_3, out_lo, out_2, out_1)

    def three(total):
        query, key, value = (total[k * part_rows : (k + 1) * part_rows] for k in range(3))
        return query.T, jnp.transpose(jnp.stack([key, value], axis=1), (1, 2, 0))

    squery, skv = three(sum_self)
    cquery, ckv = three(sum_cross)
    fin = jnp.swapaxes(jnp.stack([sum_gate, sum_up]), 1, 2)
    base = 4 * part_rows
    return (
        block_out,
        grad_tokens,
        grad_memory,
        squery,
        skv,
        sum_cross[base : base + part_rows],
        cquery,
        ckv,
        sum_cross[3 * part_rows : base],
        fin,
        sum_down,
        small[:3],
        small[3, : HEADS * LANES].reshape(HEADS, LANES)[:, : rel_bias.shape[0]].T,
    )


def solution(mesh):
    n_tok, n_mem = mesh.devices.shape
    grid = Mesh(mesh.devices.reshape(n_tok // 8, 2, 2, 2, n_mem), AXES)
    tok = AXES[:-1]
    rows = P(AXES, None)
    cols = P(None, AXES)
    deep = P(None, None, AXES)
    in_specs = (
        rows,
        rows,
        P(tok, None, None),
        P(tok, None),
        P(AXES),
        P(),
        cols,
        deep,
        rows,
        cols,
        deep,
        rows,
        deep,
        rows,
        P(),
        P(),
        rows,
    )
    out_specs = (rows, rows, rows, cols, deep, rows, cols, deep, rows, deep, rows, P(), P())
    return jax.shard_map(
        on_device, mesh=grid, in_specs=in_specs, out_specs=out_specs, check_vma=False
    )
```

```python
import jax
import jax.numpy as jnp
import numpy as np
from jax import lax
from jax.experimental import pallas as pl
from jax.experimental.pallas import tpu as pltpu
from jax.sharding import Mesh, PartitionSpec as P

HEADS = 6
HEAD_DIM = 64
INNER = HEADS * HEAD_DIM
ITEMS_DEV = 8
EPS = 1e-06
MASKED = -1e30
WIDTH = 256
LANES = 128
PAIRS = INNER // LANES
GELU_A = 0.7978845608028654
GELU_B = 0.044715
F32 = jnp.float32
BF16 = jnp.bfloat16
AXES = ("o", "a", "b", "c", "m")
GROUP = ("a", "b", "c")
VMEM = 24 * 1024 * 1024
FETCH_VMEM = 56 * 1024 * 1024


def dot_nn(left, right):
    return lax.dot_general(left, right, (((1,), (0,)), ((), ())), preferred_element_type=F32)


def dot_nt(left, right):
    return lax.dot_general(left, right, (((1,), (1,)), ((), ())), preferred_element_type=F32)


def dot_tn(left, right):
    return lax.dot_general(left, right, (((0,), (0,)), ((), ())), preferred_element_type=F32)


class Arriving:
    def __init__(self, ref, copy):
        self.ref, self.copy = ref, copy
        self.shape, self.dtype = ref.shape, ref.dtype

    def __getitem__(self, at):
        if self.copy is not None:
            self.copy.wait()
            self.copy = None
        return self.ref[at]


def kernel_call(kernel, out_shape, *args, scratch=(), scalars=0, us=5, fetch=False):
    count = len(args) - scalars
    body, extra, space = kernel, [], pltpu.VMEM
    if fetch:
        space = pl.ANY
        extra = [pltpu.VMEM(v.shape, v.dtype) for v in args] + [pltpu.SemaphoreType.DMA((count,))]

        def body(*refs):
            sources, results, held = refs[:count], refs[count : -count - 1], refs[-count - 1 : -1]
            operands = []
            for i, (source, ref) in enumerate(zip(sources, held)):
                copy = pltpu.make_async_copy(source, ref, refs[-1].at[i])
                copy.start()
                operands.append(Arriving(ref, copy))
            kernel(*operands, *results)
            for operand in operands:
                operand[...]

    return pl.pallas_call(
        body,
        out_shape=out_shape,
        in_specs=[pl.BlockSpec(memory_space=pltpu.SMEM)] * scalars
        + [pl.BlockSpec(memory_space=space)] * count,
        out_specs=jax.tree.map(lambda _: pl.BlockSpec(memory_space=pltpu.VMEM), out_shape),
        scratch_shapes=list(scratch) + extra,
        compiler_params=pltpu.CompilerParams(vmem_limit_bytes=FETCH_VMEM if fetch else VMEM),
        cost_estimate=pl.CostEstimate(flops=us * 1_000_000_000, bytes_accessed=1, transcendentals=0),
    )(*args)


def shape(*dims, kind=BF16):
    return jax.ShapeDtypeStruct(dims, kind)


def after(value, *others):
    return lax.optimization_barrier((value, *others))[0]


def lane_half(rows, side):
    lane = lax.broadcasted_iota(jnp.int32, (rows, LANES), 1)
    return (lane < HEAD_DIM) if side == 0 else (lane >= HEAD_DIM)


def pick(value, side):
    return jnp.where(lane_half(value.shape[0], side), value, jnp.zeros_like(value))


def softmax(scores):
    top = jnp.max(scores, axis=-1, keepdims=True)
    weight = jnp.exp(scores - top)
    return weight / jnp.sum(weight, axis=-1, keepdims=True)


def rms_scale(values):
    return lax.rsqrt(jnp.mean(values * values, axis=-1, keepdims=True) + EPS)


def norm_back(values, gain, grad_out):
    scale = rms_scale(values)
    weighted = grad_out * gain
    inner = jnp.mean(weighted * values, axis=-1, keepdims=True)
    grad_in = scale * weighted - values * (scale * scale * scale) * inner
    return grad_in, jnp.sum(grad_out * values * scale, axis=0, keepdims=True)


def rows_of(target_ref, at, size, first, count):
    row = lax.broadcasted_iota(jnp.int32, (count, size), 0) + first
    return (row == target_ref[:, at : at + size]).astype(F32).astype(BF16)


def to_natural(value, halves, target_ref, first, count):
    total = None
    for i, w in enumerate(halves):
        half = w.shape[0]
        hot = rows_of(target_ref, i * half, half, first, count)
        term = dot_nt(dot_nt(value, w[...]).astype(BF16), hot)
        total = term if total is None else total + term
    return total.astype(BF16)


def from_natural(value, halves, target_ref, first):
    total = None
    for i, w in enumerate(halves):
        half = w.shape[0]
        hot = rows_of(target_ref, i * half, half, first, value.shape[1])
        term = dot_nn(dot_nn(value, hot).astype(BF16), w[...])
        total = term if total is None else total + term
    return total


def shards_kernel(q_ref, kv_ref, o_ref, q2_ref, kv2_ref, o2_ref, out_ref):
    part, rows = o_ref.shape[0], out_ref.shape[0]
    r = lax.broadcasted_iota(jnp.int32, (rows, part), 0)
    i = lax.broadcasted_iota(jnp.int32, (rows, part), 1)
    total = None
    kv, kv2 = kv_ref[...], kv2_ref[...]
    shards = (q_ref[...], kv[:, 0, :], kv[:, 1, :], o_ref[...])
    shards += (q2_ref[...], kv2[:, 0, :], kv2[:, 1, :], o2_ref[...])
    for k, shard in enumerate(shards):
        hot = (r == i + k * part).astype(F32).astype(BF16)
        term = dot_nn(hot, shard)
        total = term if total is None else total + term
    out_ref[...] = total.astype(BF16)


def join_kernel(*refs):
    parts, out_ref = refs[:-1], refs[-1]
    size = parts[0].shape[0] // 2
    for i, part in enumerate(parts):
        for k in range(2):
            at = (k * len(parts) + i) * size
            out_ref[at : at + size, :] = part[k * size : (k + 1) * size, :]


def exact(left, right, dims):
    return lax.dot_general(
        left, right, (dims, ((), ())), precision=lax.Precision.HIGHEST, preferred_element_type=F32
    )


def buckets_of(lookup_ref, count):
    bucket = lax.broadcasted_iota(jnp.int32, (count, lookup_ref.shape[1]), 0)
    return (bucket == lookup_ref[...]).astype(F32)


def tables_kernel(
    m_ref, lengths_ref, runs_ref, keep_ref, peer_ref, lookup_ref, bias_ref, x_ref, gains_ref,
    ring_ref, col_ref, row_ref, slot_ref, n1_ref,
):
    m = m_ref[0]
    rows, slots = row_ref.shape[1], keep_ref.shape[1]
    for ref, axis in ((col_ref, 0), (row_ref, 1)):
        place = lax.broadcasted_iota(jnp.int32, ref.shape, axis)
        item, end = jnp.zeros(ref.shape, jnp.int32) + m * ITEMS_DEV, 0
        for i in range(ITEMS_DEV):
            end = end + lengths_ref[m, i]
            item = item + (place >= end).astype(jnp.int32)
        ref[...] = item
    for k, keep in enumerate((keep_ref, peer_ref)):
        place = lax.broadcasted_iota(jnp.int32, (1, slots), 1) + (m ^ k) * slots
        item, live, end = jnp.zeros((1, slots), jnp.int32), keep[...], 0
        for i in range(runs_ref.shape[1]):
            live = jnp.where(place == end, 1, live)
            end = end + runs_ref[0, i]
            item = item + (place >= end).astype(jnp.int32)
        slot_ref[k : k + 1, :] = jnp.where(live > 0, item, -1)
    by_distance = exact(bias_ref[...], buckets_of(lookup_ref, bias_ref.shape[0]), ((0,), (0,)))
    d = lax.broadcasted_iota(jnp.int32, (lookup_ref.shape[1], WIDTH), 0)
    k = lax.broadcasted_iota(jnp.int32, (lookup_ref.shape[1], WIDTH), 1)
    turn = ((d + k == WIDTH) | (d + k == 0)).astype(F32)
    ring_ref[...] = jnp.zeros_like(ring_ref)
    ring_ref[0:HEADS, :] = exact(by_distance, turn, ((1,), (0,)))
    x = x_ref[...].astype(F32)
    n1_ref[...] = (x * rms_scale(x) * gains_ref[0:1, :]).astype(BF16)


def self_scores(query, key, ring, allowed):
    rows = query.shape[0]
    spread = jnp.broadcast_to(ring, (rows, WIDTH))
    bias = pltpu.roll(spread, 0, 1, stride=1, stride_axis=0)[:, :rows]
    return jnp.where(allowed, dot_nt(query, key) + bias, MASKED)


def self_allowed(items_col, items_row):
    rows = items_col.shape[0]
    r = lax.broadcasted_iota(jnp.int32, (rows, rows), 0)
    q = lax.broadcasted_iota(jnp.int32, (rows, rows), 1)
    return (items_col == items_row) & (r >= q)


def self_forward_kernel(
    x_ref, n1_ref, gains_ref, w0_ref, w1_ref, target_ref, ring_ref, col_ref, row_ref,
    x2_ref, n2_ref, qkv_ref, low_ref,
):
    x = x_ref[...].astype(F32)
    n = n1_ref[...]
    halves = (w0_ref, w1_ref)
    qkv_ref[...] = to_natural(n, halves, target_ref, 0, 3 * INNER)
    allowed = self_allowed(col_ref[...], row_ref[...])
    rows = x.shape[0]
    for pair in range(PAIRS):
        at = pair * LANES
        query = qkv_ref[:, at : at + LANES]
        key = qkv_ref[:, INNER + at : INNER + at + LANES]
        value = qkv_ref[:, 2 * INNER + at : 2 * INNER + at + LANES]
        outs = []
        for side in range(2):
            h = 2 * pair + side
            probs = softmax(self_scores(pick(query, side), key, ring_ref[h : h + 1, :], allowed))
            outs.append(dot_nn(probs.astype(BF16), value))
        low_ref[:, at : at + LANES] = jnp.where(lane_half(rows, 0), outs[0], outs[1]).astype(BF16)
    x2 = x + from_natural(low_ref[...], halves, target_ref, 3 * INNER)
    x2_ref[...] = x2
    n2_ref[...] = (x2 * rms_scale(x2) * gains_ref[1:2, :]).astype(BF16)


def self_backward_kernel(
    g2_ref, x_ref, gains_ref, w0_ref, w1_ref, target_ref, plain_ref, qkv_ref, ring_ref, col_ref,
    row_ref, lookup_ref, g23_ref, gx_ref, dyt_ref, small_ref, dqkv_ref, diag_ref,
):
    halves = (w0_ref, w1_ref)
    grad = to_natural(g2_ref[...].astype(BF16), halves, target_ref, 3 * INNER, INNER)
    allowed = self_allowed(col_ref[...], row_ref[...])
    rows = x_ref.shape[0]
    diag_ref[...] = jnp.zeros_like(diag_ref)
    r = lax.broadcasted_iota(jnp.int32, (rows, rows), 0)
    q = lax.broadcasted_iota(jnp.int32, (rows, rows), 1)
    upside = (r + q == rows - 1).astype(BF16)
    for pair in range(PAIRS):
        at = pair * LANES
        query = qkv_ref[:, at : at + LANES]
        key = qkv_ref[:, INNER + at : INNER + at + LANES]
        value = qkv_ref[:, 2 * INNER + at : 2 * INNER + at + LANES]
        g_pair = grad[:, at : at + LANES]
        dq, dk, dv = [], [], []
        for side in range(2):
            h = 2 * pair + side
            probs = softmax(self_scores(pick(query, side), key, ring_ref[h : h + 1, :], allowed))
            dp = dot_nt(pick(g_pair, side), value)
            ds = probs * (dp - jnp.sum(probs * dp, axis=-1, keepdims=True))
            low = ds.astype(BF16)
            wide = jnp.concatenate(
                [dot_nn(upside, low), jnp.zeros((rows, WIDTH - rows), F32)], axis=1
            )
            turned = pltpu.roll(wide, 0, 1, stride=1, stride_axis=0)
            diag_ref[h : h + 1, :] = jnp.sum(turned, axis=0, keepdims=True)
            dq.append(dot_nn(low, key))
            dk.append(dot_tn(low, query))
            dv.append(dot_tn(probs.astype(BF16), g_pair))
        left = lane_half(rows, 0)
        for k, two in enumerate((dq, dk, dv)):
            dqkv_ref[:, k * INNER + at : k * INNER + at + LANES] = jnp.where(
                left, two[0], two[1]
            ).astype(BF16)
    plain = rows_of(plain_ref, 0, plain_ref.shape[1], 0, 3 * INNER)
    dyt_ref[...] = dot_nn(dqkv_ref[...], plain).T.astype(BF16)
    back = from_natural(dqkv_ref[...], halves, target_ref, 0)
    grad_in, gain_grad = norm_back(x_ref[...].astype(F32), gains_ref[0:1, :], back)
    gx_ref[...] = g2_ref[...] + grad_in
    small_ref[...] = jnp.zeros_like(small_ref)
    small_ref[0:1, :] = gain_grad
    small_ref[1:3, :] = g23_ref[...]
    k = lax.broadcasted_iota(jnp.int32, (WIDTH, rows), 0)
    d = lax.broadcasted_iota(jnp.int32, (WIDTH, rows), 1)
    by_distance = exact(diag_ref[...], (k + d == rows - 1).astype(F32), ((1,), (0,)))
    buckets = buckets_of(lookup_ref, LANES)
    by_bucket = exact(by_distance, buckets, ((1,), (1,)))
    for h in range(HEADS):
        small_ref[3:4, h * LANES : (h + 1) * LANES] = by_bucket[h : h + 1, :]


def memory_forward_kernel(own_ref, peer_ref, w0_ref, w1_ref, target_ref, kv_own_ref, kv_peer_ref):
    halves = (w0_ref, w1_ref)
    kv_own_ref[...] = to_natural(own_ref[...], halves, target_ref, INNER, 2 * INNER)
    kv_peer_ref[...] = to_natural(peer_ref[...], halves, target_ref, INNER, 2 * INNER)


def memory_backward_kernel(own_ref, got_ref, w0_ref, w1_ref, target_ref, out_ref):
    total = (own_ref[...].astype(F32) + got_ref[...].astype(F32)).astype(BF16)
    out_ref[...] = from_natural(total, (w0_ref, w1_ref), target_ref, INNER)


def key_value(own_ref, peer_ref, at):
    key = jnp.concatenate([r[:, at : at + LANES] for r in (own_ref, peer_ref)], axis=0)
    at += INNER
    return key, jnp.concatenate([r[:, at : at + LANES] for r in (own_ref, peer_ref)], axis=0)


def cross_forward_kernel(
    x_ref, n_ref, gains_ref, w0_ref, w1_ref, target_ref, own_ref, peer_ref, col_ref, slot_ref,
    x3_ref, n3_ref, q_ref, low_ref,
):
    halves = (w0_ref, w1_ref)
    q_ref[...] = to_natural(n_ref[...], halves, target_ref, 0, INNER)
    reach = col_ref[...] == jnp.concatenate([slot_ref[k : k + 1, :] for k in range(2)], axis=1)
    rows = x_ref.shape[0]
    for pair in range(PAIRS):
        at = pair * LANES
        query = q_ref[:, at : at + LANES]
        key, value = key_value(own_ref, peer_ref, at)
        outs = []
        for side in range(2):
            probs = softmax(jnp.where(reach, dot_nt(pick(query, side), key), MASKED))
            outs.append(dot_nn(probs.astype(BF16), value))
        low_ref[:, at : at + LANES] = jnp.where(lane_half(rows, 0), outs[0], outs[1]).astype(BF16)
    x3 = x_ref[...] + from_natural(low_ref[...], halves, target_ref, 3 * INNER)
    x3_ref[...] = x3
    n3_ref[...] = (x3 * rms_scale(x3) * gains_ref[2:3, :]).astype(BF16)


def cross_backward_kernel(
    lo_ref, got_c_ref, got_2_ref, got_ref, x3_ref, x2_ref, gains_ref, cot_ref, w0_ref, w1_ref, target_ref, q_ref,
    own_ref, peer_ref, col_ref, slot_ref, low3_ref, g2_ref, dq_ref, dkv_own_ref, dkv_peer_ref,
    gain_ref,
):
    halves = (w0_ref, w1_ref)
    rows = x3_ref.shape[0]
    grad_n3 = got_ref[...].astype(F32) + sum(
        ref[0:rows, :].astype(F32) for ref in (lo_ref, got_c_ref, got_2_ref)
    )
    grad_in, gain_3 = norm_back(x3_ref[...], gains_ref[2:3, :], grad_n3)
    grad_3 = cot_ref[...].astype(F32) + grad_in
    low3_ref[...] = grad_3.astype(BF16)
    grad = to_natural(low3_ref[...], halves, target_ref, 3 * INNER, INNER)
    reach = col_ref[...] == jnp.concatenate([slot_ref[k : k + 1, :] for k in range(2)], axis=1)
    rows = x3_ref.shape[0]
    slots = own_ref.shape[0]
    for pair in range(PAIRS):
        at = pair * LANES
        query = q_ref[:, at : at + LANES]
        key, value = key_value(own_ref, peer_ref, at)
        g_pair = grad[:, at : at + LANES]
        dq, dk, dv = [], [], []
        for side in range(2):
            probs = softmax(jnp.where(reach, dot_nt(pick(query, side), key), MASKED))
            dp = dot_nt(pick(g_pair, side), value)
            ds = (probs * (dp - jnp.sum(probs * dp, axis=-1, keepdims=True))).astype(BF16)
            dq.append(dot_nn(ds, key))
            dk.append(dot_tn(ds, query))
            dv.append(dot_tn(probs.astype(BF16), g_pair))
        dq_ref[:, at : at + LANES] = jnp.where(lane_half(rows, 0), dq[0], dq[1]).astype(BF16)
        left = lane_half(2 * slots, 0)
        for k, two in ((0, dk), (INNER, dv)):
            both = jnp.where(left, two[0], two[1]).astype(BF16)
            dkv_own_ref[:, k + at : k + at + LANES] = both[:slots]
            dkv_peer_ref[:, k + at : k + at + LANES] = both[slots:]
    back = from_natural(dq_ref[...], halves, target_ref, 0)
    grad_in, gain_2 = norm_back(x2_ref[...], gains_ref[1:2, :], back)
    g2_ref[...] = grad_3 + grad_in
    gain_ref[0:1, :] = gain_2
    gain_ref[1:2, :] = gain_3


def weights_kernel(
    dq_ref, low_ref, own_ref, peer_ref, low1_ref, n2_ref, low3_ref, mem_own_ref, mem_peer_ref, g2_ref,
    target_ref, one_ref, *out_refs,
):
    right = jnp.concatenate([n2_ref[...], low3_ref[...], mem_own_ref[...], mem_peer_ref[...]], axis=0)
    right_out = g2_ref[...].astype(BF16)
    for i, out_ref in enumerate(out_refs):

        def spread(order_ref, first, value):
            size = order_ref.shape[1] // 2
            hot = rows_of(order_ref, i * size, size, first, value.shape[1])
            return dot_nn(value, hot).astype(BF16)

        left = jnp.concatenate(
            [
                spread(target_ref, 0, dq_ref[...]),
                spread(target_ref, 3 * INNER, low_ref[...]),
                spread(target_ref, INNER, own_ref[...]),
                spread(target_ref, INNER, peer_ref[...]),
            ],
            axis=0,
        )
        cross = dot_tn(left, right).astype(BF16)
        out = dot_tn(spread(one_ref, 0, low1_ref[...]), right_out).astype(BF16)
        wide, slim = cross.shape[0] // 4, out.shape[0] // 4
        for k in range(4):
            at = k * (wide + slim)
            out_ref[at : at + wide, :] = cross[k * wide : (k + 1) * wide]
            out_ref[at + wide : at + wide + slim, :] = out[k * slim : (k + 1) * slim]


def columns_kernel(at_ref, held_ref, lo_ref, hi_ref, out_ref):
    rows = held_ref.shape[2]
    total = None
    for k in range(8):
        right = (lo_ref if k < 4 else hi_ref)[(k % 4) * rows : (k % 4 + 1) * rows, :]
        term = dot_nn(held_ref[at_ref[k]], right)
        total = term if total is None else total + term
    out_ref[...] = total.astype(BF16)


def assemble(parts, whole_ref):
    cols = parts[0].shape[0]
    for i, part in enumerate(parts):
        whole_ref[i * cols : (i + 1) * cols, :] = part[...]


def grad_hidden_kernel(c_ref, *refs):
    parts, out_ref, wd_ref = refs[:-2], refs[-2], refs[-1]
    assemble(parts, wd_ref)
    out_ref[...] = dot_nt(c_ref[...], wd_ref[...])


def ffn_kernel(n_ref, gh_ref, *refs):
    parts, (h_ref, dg_ref, du_ref, gn_ref, wg_ref, wu_ref) = refs[:-6], refs[-6:]
    assemble(parts[: len(parts) // 2], wg_ref)
    assemble(parts[len(parts) // 2 :], wu_ref)
    n = n_ref[...]
    gate = dot_nt(n, wg_ref[...])
    up = dot_nt(n, wu_ref[...])
    square = gate * gate
    t = jnp.tanh(GELU_A * gate * (1.0 + GELU_B * square))
    half = 0.5 * (1.0 + t)
    act = gate * half
    h_ref[...] = (act * up).astype(BF16)
    gh = gh_ref[...]
    slope = half + 0.5 * gate * (1.0 - t * t) * (GELU_A * (1.0 + 3.0 * GELU_B * square))
    d_gate = (gh * up * slope).astype(BF16)
    d_up = (gh * act).astype(BF16)
    dg_ref[...] = d_gate
    du_ref[...] = d_up
    gn_ref[...] = (dot_nn(d_gate, wg_ref[...]) + dot_nn(d_up, wu_ref[...])).astype(BF16)


def ffn_out_kernel(h_ref, *refs):
    parts, out_ref, wd_ref = refs[:-2], refs[-2], refs[-1]
    got_ref, parts = (parts[0], parts[1:]) if len(parts) % 2 else (None, parts)
    assemble(parts, wd_ref)
    value = dot_nn(h_ref[...], wd_ref[...])
    if got_ref is not None:
        value = value + got_ref[...].astype(F32)
    out_ref[...] = value.astype(BF16)


def ffn_weights_kernel(
    h0_ref, h1_ref, g0_ref, g1_ref, u0_ref, u1_ref, n0_ref, n1_ref, c0_ref, c1_ref, *out_refs
):
    sets = (
        ((h0_ref, c0_ref), (h1_ref, c1_ref)),
        ((g0_ref, n0_ref), (g1_ref, n1_ref)),
        ((u0_ref, n0_ref), (u1_ref, n1_ref)),
    )
    for out_ref, pairs in zip(out_refs, sets):
        out_ref[...] = sum(dot_tn(left[...], right[...]) for left, right in pairs).astype(BF16)


def on_device(
    tokens,
    memory,
    target_lengths,
    memory_lengths,
    keep_mask,
    distance_bucket_lookup,
    self_query,
    self_kv,
    self_out,
    cross_query,
    cross_key_value,
    cross_out,
    ffn_in,
    ffn_down,
    norm_gains,
    rel_bias,
    cotangent,
):
    size = {axis: lax.axis_size(axis) for axis in AXES}
    me = {axis: lax.axis_index(axis) for axis in AXES}
    rows, width = tokens.shape
    slots = memory.shape[0]
    part_rows, ff_rows = self_out.shape[0], ffn_down.shape[0]
    n_o = size["o"]
    quads = 2 * n_o

    def cut(value):
        if value.ndim < 2 or value.shape[-2] % LANES:
            return value
        return value.reshape(*value.shape[:-2], -1, LANES // 2, value.shape[-1])

    def permute(value, move):
        pairs = []
        for flat in range(quads * 8):
            rest, at = flat, {}
            for axis in reversed(AXES):
                at[axis], rest = rest % size[axis], rest // size[axis]
            to = move(dict(at))
            there = 0
            for axis in AXES:
                there = there * size[axis] + to[axis]
            pairs.append((flat, there))
        return lax.ppermute(cut(value), AXES, pairs).reshape(value.shape)

    def flips(**masks):
        def move(at):
            return {axis: at[axis] ^ masks.get(axis, 0) for axis in AXES}

        return move

    def flip_by_core(first, second):
        def move(at):
            at[first if at["c"] == 0 else second] ^= 1
            return at

        return move

    first_move, second_move = flip_by_core("b", "a"), flip_by_core("a", "b")
    core_move, peer_move = flips(c=1), flips(m=1)

    def grow(held, move):
        return jnp.concatenate([held, permute(held, move)], axis=0)

    def exchange(value, axes, parts):
        value = value.reshape(parts, -1, value.shape[-1])
        got = lax.all_to_all(cut(value), axes, split_axis=0, concat_axis=0, tiled=True)
        return got.reshape(value.shape)

    stage = lax.optimization_barrier
    full, slim = (rows, width), (rows, INNER)
    half, cols = 4 * rows, quads * ff_rows
    kv_shape = shape(slots, 2 * INNER)
    down, gate, up = (pltpu.VMEM((cols, width), BF16) for _ in range(3))

    def flat_of(at):
        return ((((at["o"] * 2 + at["a"]) * 2 + at["b"]) * 2 + at["c"]) * 2) + at["m"]

    def mask_of(eighth, quad, core):
        by_1, by_2 = ("b", "a") if core ^ (eighth // 4) == 0 else ("a", "b")
        at = {"o": quad % n_o, "m": quad // n_o, "c": eighth // 4}
        at[by_1], at[by_2] = eighth % 2, (eighth // 2) % 2
        return flat_of(at)

    masks = np.array(
        [[mask_of(e, q, core) for e in range(8) for q in range(quads)] for core in range(2)]
    ).astype(np.int32)
    piece = 4 * part_rows

    def target_of(owner, padded):
        row = np.arange(padded)
        base = row // part_rows * INNER + row % part_rows
        return owner[:, None] * part_rows + base[None, :].astype(np.int32)

    moves = [flips(o=k % n_o, m=k // n_o) for k in range(1, quads)]
    wide = quads * piece

    own_both = kernel_call(
        shards_kernel, shape(2 * piece, width), self_query.T, jnp.transpose(self_kv, (2, 0, 1)), self_out,
        cross_query.T, jnp.transpose(cross_key_value, (2, 0, 1)), cross_out, us=2, fetch=True,
    )
    got = [own_both] + [permute(own_both, move) for move in moves]
    here, at_core = after((flat_of(me), me["c"]), own_both)
    mask = jnp.where(at_core == 0, masks[0], masks[1])
    target = target_of(here ^ mask, piece).reshape(1, -1)
    one = jnp.where(
        np.arange(16)[None, :] < part_rows, target_of(here ^ mask, 16), -1
    ).reshape(1, -1)
    om_bits = flat_of({"o": n_o - 1, "a": 0, "b": 0, "c": 0, "m": 1})
    quad_masks = masks[0, :quads]
    owner = (np.arange(8, dtype=np.int32)[:, None] * 2) | ((here & om_bits) ^ quad_masks)[None, :]
    plain = target_of(owner.reshape(-1), 40).reshape(1, -1)
    eight_at = ((here ^ mask[::quads]) // 2) % 8
    both = kernel_call(join_kernel, shape(2 * quads * piece, width), *got, us=1)
    cot_1 = grow(cotangent, first_move)
    keep = keep_mask.reshape(1, -1)
    peer_keep = permute(keep, peer_move)
    own_gate, own_up = jnp.swapaxes(ffn_in, 1, 2)

    def two_halves(held, got):
        half = held.shape[0] // 2
        return [jnp.concatenate([held[at : at + half], got[at : at + half]], axis=0) for at in (0, half)]

    both, cot_1, peer_keep, memory, target, one, plain, eight_at, own_down = stage(
        (both, cot_1, peer_keep, memory, target, one, plain, eight_at, ffn_down)
    )
    both = jnp.concatenate(two_halves(both, permute(both, first_move)), axis=0)
    peer_memory = permute(memory, peer_move)
    lookup = distance_bucket_lookup.reshape(1, -1)
    ring, items_col, items_row, slot, own_1 = kernel_call(
        tables_kernel,
        [
            shape(8, WIDTH, kind=F32), shape(rows, 1, kind=jnp.int32), shape(1, rows, kind=jnp.int32),
            shape(2, slots, kind=jnp.int32), shape(*full),
        ],
        me["m"].reshape(1), target_lengths[0], memory_lengths, keep, peer_keep, lookup, rel_bias,
        tokens, norm_gains, scalars=3,
    )

    def over_o(own):
        return [own] + [permute(own, flips(o=k)) for k in range(1, n_o)]

    def over_m(parts, own_m):
        return parts + [own_m] + [permute(v, peer_move) for v in parts[1:]]

    down_o, down_m = over_o(own_down), permute(own_down, peer_move)

    both, ring, own_1, own_gate, down_o, down_m = stage(
        (both, ring, own_1, own_gate, down_o, down_m)
    )
    self_lo, cross_lo = two_halves(both, permute(both, second_move))
    gate_o, gate_m = over_o(own_gate), permute(own_gate, peer_move)
    w_down = over_m(down_o, down_m)

    self_lo, cross_lo, peer_memory, gate_o, gate_m, target, w_down, own_up = stage(
        (self_lo, cross_lo, peer_memory, gate_o, gate_m, target, w_down, own_up)
    )
    up_o, up_m = over_o(own_up), permute(own_up, peer_move)
    w_self = (self_lo, permute(self_lo, core_move))
    w_cross = (cross_lo, permute(cross_lo, core_move))

    w_self, w_cross, cot_1, gate_o = stage((w_self, w_cross, cot_1, gate_o))
    x_2, n_2, qkv, low_1 = kernel_call(
        self_forward_kernel,
        [shape(*full, kind=F32), shape(*full), shape(rows, 3 * INNER), shape(*slim)],
        tokens, own_1, norm_gains, *w_self, target, ring, items_col, items_row,
    )
    kv_own, kv_peer = kernel_call(
        memory_forward_kernel, [kv_shape] * 2, memory, peer_memory, *w_cross, target
    )
    x_3, n_3, q_2, low_2 = kernel_call(
        cross_forward_kernel,
        [shape(*full, kind=F32), shape(*full), shape(*slim), shape(*slim)],
        x_2, n_2, norm_gains, *w_cross, target, kv_own, kv_peer, items_col, slot,
    )
    cot_lo = grow(cot_1, second_move)
    w_gate = over_m(gate_o, gate_m)

    x_3, n_3, cot_lo, w_gate, up_o, up_m = stage((x_3, n_3, cot_lo, w_gate, up_o, up_m))
    w_up = over_m(up_o, up_m)
    n_1 = grow(n_3, first_move)
    cot_hi = permute(cot_lo, core_move)

    def grad_hidden(value):
        return kernel_call(
            grad_hidden_kernel, shape(half, cols, kind=F32), value, *w_down, scratch=[down], us=2
        )

    gh_lo = grad_hidden(cot_lo)

    n_1, cot_hi, gh_lo, own_1, w_up = stage((n_1, cot_hi, gh_lo, own_1, w_up))
    n_lo = grow(n_1, second_move)
    gh_hi = grad_hidden(cot_hi)

    def ffn(value, gh):
        return kernel_call(
            ffn_kernel,
            [shape(half, cols), shape(half, cols), shape(half, cols), shape(half, width)],
            value, gh, *w_gate, *w_up, scratch=[gate, up],
        )

    n_lo, gh_hi, own_1 = stage((n_lo, gh_hi, own_1))
    n_hi = permute(n_lo, core_move)
    lo_f = ffn(n_lo, gh_lo)
    one_1 = grow(own_1, first_move)

    n_hi, lo_f = stage((n_hi, lo_f))
    hi_f = ffn(n_hi, gh_hi)

    (h_lo, g_lo, u_lo, gn_lo), (h_hi, g_hi, u_hi, gn_hi) = stage((lo_f, hi_f))
    got_c = permute(gn_hi, core_move)

    def ffn_out(*args):
        return kernel_call(
            ffn_out_kernel, shape(half, width), *args, *w_down, scratch=[down], us=2
        )

    out_hi = ffn_out(h_hi)

    def summed(at, end, *parts):
        return sum(v[at:end].astype(F32) for v in parts).astype(BF16)

    got_c, out_hi, h_lo = stage((got_c, out_hi, h_lo))
    got_2 = permute(summed(2 * rows, 4 * rows, gn_lo, got_c), second_move)
    out_got = permute(out_hi, core_move)
    grad_down, grad_gate, grad_up = kernel_call(
        ffn_weights_kernel,
        [shape(cols, width)] * 3,
        h_lo, h_hi, g_lo, g_hi, u_lo, u_hi, n_lo, n_hi, cot_lo, cot_hi,
    )

    got_2, out_got, grad_down = stage((got_2, out_got, grad_down))
    got_1 = permute(summed(rows, 2 * rows, gn_lo, got_c, got_2), first_move)
    out_lo = ffn_out(h_lo, out_got)

    def over_m_back(grad):
        return permute(grad[cols // 2 :], peer_move)

    def over_o_back(grad, got):
        return [
            permute(summed(k * ff_rows, (k + 1) * ff_rows, grad, got), flips(o=k))
            for k in range(1, n_o)
        ]

    def back_sum(part, *parts):
        return sum(v[:part].astype(F32) for v in parts)

    down_m = over_m_back(grad_down)

    got_1, out_lo, one_1 = stage((got_1, out_lo, one_1))
    low_3, grad_2, dq, dkv_own, dkv_peer, gains_23 = kernel_call(
        cross_backward_kernel,
        [
            shape(*full), shape(*full, kind=F32), shape(*slim), kv_shape, kv_shape,
            shape(2, width, kind=F32),
        ],
        gn_lo, got_c, got_2, got_1, x_3, x_2, norm_gains, cotangent, *w_cross, target, q_2, kv_own,
        kv_peer, items_col, slot, us=8,
    )
    n1_lo = grow(one_1, second_move)

    grad_2, dq, down_m, grad_gate, dkv_peer = stage((grad_2, dq, down_m, grad_gate, dkv_peer))
    grad_tokens, dyt, small = kernel_call(
        self_backward_kernel,
        [shape(*full, kind=F32), shape(8 * quads * 40, rows), shape(4, width, kind=F32)],
        grad_2, tokens, norm_gains, *w_self, target, plain, qkv, ring, items_col, items_row, lookup,
        gains_23, scratch=[pltpu.VMEM((rows, 3 * INNER), BF16), pltpu.VMEM((8, WIDTH), F32)], us=8,
    )
    gate_m = over_m_back(grad_gate)

    grad_tokens, dyt, small, n1_lo, down_m = stage((grad_tokens, dyt, small, n1_lo, down_m))
    held = exchange(dyt, GROUP, 8)
    stack = shape(4 * quads * (piece + 16), width)
    kept, sent = kernel_call(
        weights_kernel, [stack] * 2,
        dq, low_2, dkv_own, dkv_peer, low_1, n_2, low_3, memory, peer_memory, grad_2, target, one, us=10,
    )
    n1_hi = permute(n1_lo, core_move)
    small = small + permute(small, core_move)
    down_b = over_o_back(grad_down, down_m)
    out_2 = permute(out_lo[2 * rows :], second_move)

    held, sent, small, n1_hi, gate_m, grad_up, out_2, dkv_peer, down_b = stage(
        (held, sent, small, n1_hi, gate_m, grad_up, out_2, dkv_peer, down_b)
    )
    cross_c = permute(sent, core_move)
    part_self = kernel_call(
        columns_kernel, shape(quads * 40, width), eight_at, held, n1_lo, n1_hi, scalars=1, us=2
    )
    self_got = [permute(part_self[k * 40 + 40 : k * 40 + 80], move) for k, move in enumerate(moves)]
    small = small + permute(small, second_move)
    out_1 = permute(summed(rows, 2 * rows, out_lo, out_2), first_move)
    up_m = over_m_back(grad_up)
    dkv_got = permute(dkv_peer, peer_move)

    cross_c, part_self, small, gate_m, dkv_got, out_1 = stage(
        (cross_c, part_self, small, gate_m, dkv_got, out_1)
    )
    gate_b = over_o_back(grad_gate, gate_m)
    block_out = summed(0, rows, x_3, out_lo, out_2, out_1)
    quarter = kept.shape[0] // 4
    cross_2 = permute(summed(2 * quarter, 4 * quarter, kept, cross_c), second_move)
    small = small + permute(small, first_move)
    sum_down = back_sum(ff_rows, grad_down, down_m, *down_b)

    cross_2, self_got, small, up_m, dkv_got, sum_down, block_out, gate_b = stage(
        (cross_2, self_got, small, up_m, dkv_got, sum_down, block_out, gate_b)
    )
    sum_gate = back_sum(ff_rows, grad_gate, gate_m, *gate_b)
    cross_1 = permute(summed(quarter, 2 * quarter, kept, cross_c, cross_2), first_move)
    small_got = [permute(small, move) for move in moves]
    up_b = over_o_back(grad_up, up_m)
    grad_memory = kernel_call(
        memory_backward_kernel, shape(slots, width, kind=F32), dkv_own, dkv_got, *w_cross, target
    )
    sum_self = back_sum(40, part_self, *self_got)

    cross_1, small_got, sum_self, grad_memory, sum_gate = stage(
        (cross_1, small_got, sum_self, grad_memory, sum_gate)
    )

    def pieces(k):
        return jnp.concatenate(
            [
                sum(v[at:end].astype(F32) for v in (kept, cross_c, cross_2, cross_1))
                for at, end in ((k * piece, k * piece + piece), (wide + k * 16, wide + k * 16 + 16))
            ],
            axis=0,
        )

    pieces_got = [permute(pieces(k + 1).astype(BF16), move) for k, move in enumerate(moves)]
    small = small + sum(small_got)

    pieces_got, up_b, small = stage((pieces_got, up_b, small))
    sum_cross = pieces(0) + sum(g.astype(F32) for g in pieces_got)
    sum_up = back_sum(ff_rows, grad_up, up_m, *up_b)

    def three(total):
        query, key, value = (total[k * part_rows : (k + 1) * part_rows] for k in range(3))
        return query.T, jnp.transpose(jnp.stack([key, value], axis=1), (1, 2, 0))

    squery, skv = three(sum_self)
    cquery, ckv = three(sum_cross)
    fin = jnp.swapaxes(jnp.stack([sum_gate, sum_up]), 1, 2)
    base = 4 * part_rows
    return (
        block_out,
        grad_tokens,
        grad_memory,
        squery,
        skv,
        sum_cross[base : base + part_rows],
        cquery,
        ckv,
        sum_cross[3 * part_rows : base],
        fin,
        sum_down,
        small[:3],
        small[3, : HEADS * LANES].reshape(HEADS, LANES)[:, : rel_bias.shape[0]].T,
    )


def solution(mesh):
    n_tok, n_mem = mesh.devices.shape
    grid = Mesh(mesh.devices.reshape(n_tok // 8, 2, 2, 2, n_mem), AXES)
    tok = AXES[:-1]
    rows = P(AXES, None)
    cols = P(None, AXES)
    deep = P(None, None, AXES)
    in_specs = (
        rows,
        rows,
        P(tok, None, None),
        P(tok, None),
        P(AXES),
        P(),
        cols,
        deep,
        rows,
        cols,
        deep,
        rows,
        deep,
        rows,
        P(),
        P(),
        rows,
    )
    out_specs = (rows, rows, rows, cols, deep, rows, cols, deep, rows, deep, rows, P(), P())
    return jax.shard_map(
        on_device, mesh=grid, in_specs=in_specs, out_specs=out_specs, check_vma=False
    )
```

```python
import jax
import jax.numpy as jnp
import numpy as np
from jax import lax
from jax.experimental import pallas as pl
from jax.experimental.pallas import tpu as pltpu
from jax.sharding import Mesh, PartitionSpec as P

HEADS = 6
HEAD_DIM = 64
INNER = HEADS * HEAD_DIM
ITEMS_DEV = 8
EPS = 1e-06
MASKED = -1e30
WIDTH = 256
LANES = 128
PAIRS = INNER // LANES
GELU_A = 0.7978845608028654
GELU_B = 0.044715
F32 = jnp.float32
BF16 = jnp.bfloat16
AXES = ("o", "a", "b", "c", "m")
GROUP = ("a", "b", "c")
VMEM = 24 * 1024 * 1024
FETCH_VMEM = 56 * 1024 * 1024


def dot_nn(left, right):
    return lax.dot_general(left, right, (((1,), (0,)), ((), ())), preferred_element_type=F32)


def dot_nt(left, right):
    return lax.dot_general(left, right, (((1,), (1,)), ((), ())), preferred_element_type=F32)


def dot_tn(left, right):
    return lax.dot_general(left, right, (((0,), (0,)), ((), ())), preferred_element_type=F32)


class Arriving:
    def __init__(self, ref, copy):
        self.ref, self.copy = ref, copy
        self.shape, self.dtype = ref.shape, ref.dtype

    def __getitem__(self, at):
        if self.copy is not None:
            self.copy.wait()
            self.copy = None
        return self.ref[at]


def kernel_call(kernel, out_shape, *args, scratch=(), scalars=0, us=5, fetch=False):
    count = len(args) - scalars
    body, extra, space = kernel, [], pltpu.VMEM
    if fetch:
        space = pl.ANY
        extra = [pltpu.VMEM(v.shape, v.dtype) for v in args] + [pltpu.SemaphoreType.DMA((count,))]

        def body(*refs):
            sources, results, held = refs[:count], refs[count : -count - 1], refs[-count - 1 : -1]
            operands = []
            for i, (source, ref) in enumerate(zip(sources, held)):
                copy = pltpu.make_async_copy(source, ref, refs[-1].at[i])
                copy.start()
                operands.append(Arriving(ref, copy))
            kernel(*operands, *results)
            for operand in operands:
                operand[...]

    return pl.pallas_call(
        body,
        out_shape=out_shape,
        in_specs=[pl.BlockSpec(memory_space=pltpu.SMEM)] * scalars
        + [pl.BlockSpec(memory_space=space)] * count,
        out_specs=jax.tree.map(lambda _: pl.BlockSpec(memory_space=pltpu.VMEM), out_shape),
        scratch_shapes=list(scratch) + extra,
        compiler_params=pltpu.CompilerParams(vmem_limit_bytes=FETCH_VMEM if fetch else VMEM),
        cost_estimate=pl.CostEstimate(flops=us * 1_000_000_000, bytes_accessed=1, transcendentals=0),
    )(*args)


def shape(*dims, kind=BF16):
    return jax.ShapeDtypeStruct(dims, kind)


def after(value, *others):
    return lax.optimization_barrier((value, *others))[0]


def lane_half(rows, side):
    lane = lax.broadcasted_iota(jnp.int32, (rows, LANES), 1)
    return (lane < HEAD_DIM) if side == 0 else (lane >= HEAD_DIM)


def pick(value, side):
    return jnp.where(lane_half(value.shape[0], side), value, jnp.zeros_like(value))


def softmax(scores):
    top = jnp.max(scores, axis=-1, keepdims=True)
    weight = jnp.exp(scores - top)
    return weight / jnp.sum(weight, axis=-1, keepdims=True)


def rms_scale(values):
    return lax.rsqrt(jnp.mean(values * values, axis=-1, keepdims=True) + EPS)


def norm_back(values, gain, grad_out):
    scale = rms_scale(values)
    weighted = grad_out * gain
    inner = jnp.mean(weighted * values, axis=-1, keepdims=True)
    grad_in = scale * weighted - values * (scale * scale * scale) * inner
    return grad_in, jnp.sum(grad_out * values * scale, axis=0, keepdims=True)


def rows_of(target_ref, at, size, first, count):
    row = lax.broadcasted_iota(jnp.int32, (count, size), 0) + first
    return (row == target_ref[:, at : at + size]).astype(F32).astype(BF16)


def to_natural(value, halves, target_ref, first, count):
    total = None
    for i, w in enumerate(halves):
        half = w.shape[0]
        hot = rows_of(target_ref, i * half, half, first, count)
        term = dot_nt(dot_nt(value, w[...]).astype(BF16), hot)
        total = term if total is None else total + term
    return total.astype(BF16)


def from_natural(value, halves, target_ref, first):
    total = None
    for i, w in enumerate(halves):
        half = w.shape[0]
        hot = rows_of(target_ref, i * half, half, first, value.shape[1])
        term = dot_nn(dot_nn(value, hot).astype(BF16), w[...])
        total = term if total is None else total + term
    return total


def shards_kernel(q_ref, kv_ref, o_ref, q2_ref, kv2_ref, o2_ref, out_ref):
    part, rows = o_ref.shape[0], out_ref.shape[0]
    r = lax.broadcasted_iota(jnp.int32, (rows, part), 0)
    i = lax.broadcasted_iota(jnp.int32, (rows, part), 1)
    total = None
    kv, kv2 = kv_ref[...], kv2_ref[...]
    shards = (q_ref[...], kv[:, 0, :], kv[:, 1, :], o_ref[...])
    shards += (q2_ref[...], kv2[:, 0, :], kv2[:, 1, :], o2_ref[...])
    for k, shard in enumerate(shards):
        hot = (r == i + k * part).astype(F32).astype(BF16)
        term = dot_nn(hot, shard)
        total = term if total is None else total + term
    out_ref[...] = total.astype(BF16)


def join_kernel(*refs):
    parts, out_ref = refs[:-1], refs[-1]
    size = parts[0].shape[0] // 2
    for i, part in enumerate(parts):
        for k in range(2):
            at = (k * len(parts) + i) * size
            out_ref[at : at + size, :] = part[k * size : (k + 1) * size, :]


def exact(left, right, dims):
    return lax.dot_general(
        left, right, (dims, ((), ())), precision=lax.Precision.HIGHEST, preferred_element_type=F32
    )


def buckets_of(lookup_ref, count):
    bucket = lax.broadcasted_iota(jnp.int32, (count, lookup_ref.shape[1]), 0)
    return (bucket == lookup_ref[...]).astype(F32)


def tables_kernel(
    m_ref, lengths_ref, runs_ref, keep_ref, peer_ref, lookup_ref, bias_ref, x_ref, gains_ref,
    ring_ref, col_ref, row_ref, slot_ref, n1_ref,
):
    m = m_ref[0]
    rows, slots = row_ref.shape[1], keep_ref.shape[1]
    for ref, axis in ((col_ref, 0), (row_ref, 1)):
        place = lax.broadcasted_iota(jnp.int32, ref.shape, axis)
        item, end = jnp.zeros(ref.shape, jnp.int32) + m * ITEMS_DEV, 0
        for i in range(ITEMS_DEV):
            end = end + lengths_ref[m, i]
            item = item + (place >= end).astype(jnp.int32)
        ref[...] = item
    for k, keep in enumerate((keep_ref, peer_ref)):
        place = lax.broadcasted_iota(jnp.int32, (1, slots), 1) + (m ^ k) * slots
        item, live, end = jnp.zeros((1, slots), jnp.int32), keep[...], 0
        for i in range(runs_ref.shape[1]):
            live = jnp.where(place == end, 1, live)
            end = end + runs_ref[0, i]
            item = item + (place >= end).astype(jnp.int32)
        slot_ref[k : k + 1, :] = jnp.where(live > 0, item, -1)
    by_distance = exact(bias_ref[...], buckets_of(lookup_ref, bias_ref.shape[0]), ((0,), (0,)))
    d = lax.broadcasted_iota(jnp.int32, (lookup_ref.shape[1], WIDTH), 0)
    k = lax.broadcasted_iota(jnp.int32, (lookup_ref.shape[1], WIDTH), 1)
    turn = ((d + k == WIDTH) | (d + k == 0)).astype(F32)
    ring_ref[...] = jnp.zeros_like(ring_ref)
    ring_ref[0:HEADS, :] = exact(by_distance, turn, ((1,), (0,)))
    x = x_ref[...].astype(F32)
    n1_ref[...] = (x * rms_scale(x) * gains_ref[0:1, :]).astype(BF16)


def self_scores(query, key, ring, allowed):
    rows = query.shape[0]
    spread = jnp.broadcast_to(ring, (rows, WIDTH))
    bias = pltpu.roll(spread, 0, 1, stride=1, stride_axis=0)[:, :rows]
    return jnp.where(allowed, dot_nt(query, key) + bias, MASKED)


def self_allowed(items_col, items_row):
    rows = items_col.shape[0]
    r = lax.broadcasted_iota(jnp.int32, (rows, rows), 0)
    q = lax.broadcasted_iota(jnp.int32, (rows, rows), 1)
    return (items_col == items_row) & (r >= q)


def self_forward_kernel(
    x_ref, n1_ref, gains_ref, w0_ref, w1_ref, target_ref, ring_ref, col_ref, row_ref,
    x2_ref, n2_ref, qkv_ref, low_ref,
):
    x = x_ref[...].astype(F32)
    n = n1_ref[...]
    halves = (w0_ref, w1_ref)
    qkv_ref[...] = to_natural(n, halves, target_ref, 0, 3 * INNER)
    allowed = self_allowed(col_ref[...], row_ref[...])
    rows = x.shape[0]
    for pair in range(PAIRS):
        at = pair * LANES
        query = qkv_ref[:, at : at + LANES]
        key = qkv_ref[:, INNER + at : INNER + at + LANES]
        value = qkv_ref[:, 2 * INNER + at : 2 * INNER + at + LANES]
        outs = []
        for side in range(2):
            h = 2 * pair + side
            probs = softmax(self_scores(pick(query, side), key, ring_ref[h : h + 1, :], allowed))
            outs.append(dot_nn(probs.astype(BF16), value))
        low_ref[:, at : at + LANES] = jnp.where(lane_half(rows, 0), outs[0], outs[1]).astype(BF16)
    x2 = x + from_natural(low_ref[...], halves, target_ref, 3 * INNER)
    x2_ref[...] = x2
    n2_ref[...] = (x2 * rms_scale(x2) * gains_ref[1:2, :]).astype(BF16)


def self_backward_kernel(
    g2_ref, x_ref, gains_ref, w0_ref, w1_ref, target_ref, plain_ref, qkv_ref, ring_ref, col_ref,
    row_ref, lookup_ref, g23_ref, gx_ref, dyt_ref, small_ref, dqkv_ref, diag_ref,
):
    halves = (w0_ref, w1_ref)
    grad = to_natural(g2_ref[...].astype(BF16), halves, target_ref, 3 * INNER, INNER)
    allowed = self_allowed(col_ref[...], row_ref[...])
    rows = x_ref.shape[0]
    diag_ref[...] = jnp.zeros_like(diag_ref)
    r = lax.broadcasted_iota(jnp.int32, (rows, rows), 0)
    q = lax.broadcasted_iota(jnp.int32, (rows, rows), 1)
    upside = (r + q == rows - 1).astype(BF16)
    for pair in range(PAIRS):
        at = pair * LANES
        query = qkv_ref[:, at : at + LANES]
        key = qkv_ref[:, INNER + at : INNER + at + LANES]
        value = qkv_ref[:, 2 * INNER + at : 2 * INNER + at + LANES]
        g_pair = grad[:, at : at + LANES]
        dq, dk, dv = [], [], []
        for side in range(2):
            h = 2 * pair + side
            probs = softmax(self_scores(pick(query, side), key, ring_ref[h : h + 1, :], allowed))
            dp = dot_nt(pick(g_pair, side), value)
            ds = probs * (dp - jnp.sum(probs * dp, axis=-1, keepdims=True))
            low = ds.astype(BF16)
            wide = jnp.concatenate(
                [dot_nn(upside, low), jnp.zeros((rows, WIDTH - rows), F32)], axis=1
            )
            turned = pltpu.roll(wide, 0, 1, stride=1, stride_axis=0)
            diag_ref[h : h + 1, :] = jnp.sum(turned, axis=0, keepdims=True)
            dq.append(dot_nn(low, key))
            dk.append(dot_tn(low, query))
            dv.append(dot_tn(probs.astype(BF16), g_pair))
        left = lane_half(rows, 0)
        for k, two in enumerate((dq, dk, dv)):
            dqkv_ref[:, k * INNER + at : k * INNER + at + LANES] = jnp.where(
                left, two[0], two[1]
            ).astype(BF16)
    plain = rows_of(plain_ref, 0, plain_ref.shape[1], 0, 3 * INNER)
    dyt_ref[...] = dot_nn(dqkv_ref[...], plain).T.astype(BF16)
    back = from_natural(dqkv_ref[...], halves, target_ref, 0)
    grad_in, gain_grad = norm_back(x_ref[...].astype(F32), gains_ref[0:1, :], back)
    gx_ref[...] = g2_ref[...] + grad_in
    small_ref[...] = jnp.zeros_like(small_ref)
    small_ref[0:1, :] = gain_grad
    small_ref[1:3, :] = g23_ref[...]
    k = lax.broadcasted_iota(jnp.int32, (WIDTH, rows), 0)
    d = lax.broadcasted_iota(jnp.int32, (WIDTH, rows), 1)
    by_distance = exact(diag_ref[...], (k + d == rows - 1).astype(F32), ((1,), (0,)))
    buckets = buckets_of(lookup_ref, LANES)
    by_bucket = exact(by_distance, buckets, ((1,), (1,)))
    for h in range(HEADS):
        small_ref[3:4, h * LANES : (h + 1) * LANES] = by_bucket[h : h + 1, :]


def memory_forward_kernel(own_ref, peer_ref, w0_ref, w1_ref, target_ref, kv_own_ref, kv_peer_ref):
    halves = (w0_ref, w1_ref)
    kv_own_ref[...] = to_natural(own_ref[...], halves, target_ref, INNER, 2 * INNER)
    kv_peer_ref[...] = to_natural(peer_ref[...], halves, target_ref, INNER, 2 * INNER)


def memory_backward_kernel(own_ref, got_ref, w0_ref, w1_ref, target_ref, out_ref):
    total = (own_ref[...].astype(F32) + got_ref[...].astype(F32)).astype(BF16)
    out_ref[...] = from_natural(total, (w0_ref, w1_ref), target_ref, INNER)


def key_value(own_ref, peer_ref, at):
    key = jnp.concatenate([r[:, at : at + LANES] for r in (own_ref, peer_ref)], axis=0)
    at += INNER
    return key, jnp.concatenate([r[:, at : at + LANES] for r in (own_ref, peer_ref)], axis=0)


def cross_forward_kernel(
    x_ref, n_ref, gains_ref, w0_ref, w1_ref, target_ref, own_ref, peer_ref, col_ref, slot_ref,
    x3_ref, n3_ref, q_ref, low_ref,
):
    halves = (w0_ref, w1_ref)
    q_ref[...] = to_natural(n_ref[...], halves, target_ref, 0, INNER)
    reach = col_ref[...] == jnp.concatenate([slot_ref[k : k + 1, :] for k in range(2)], axis=1)
    rows = x_ref.shape[0]
    for pair in range(PAIRS):
        at = pair * LANES
        query = q_ref[:, at : at + LANES]
        key, value = key_value(own_ref, peer_ref, at)
        outs = []
        for side in range(2):
            probs = softmax(jnp.where(reach, dot_nt(pick(query, side), key), MASKED))
            outs.append(dot_nn(probs.astype(BF16), value))
        low_ref[:, at : at + LANES] = jnp.where(lane_half(rows, 0), outs[0], outs[1]).astype(BF16)
    x3 = x_ref[...] + from_natural(low_ref[...], halves, target_ref, 3 * INNER)
    x3_ref[...] = x3
    n3_ref[...] = (x3 * rms_scale(x3) * gains_ref[2:3, :]).astype(BF16)


def cross_backward_kernel(
    lo_ref, got_c_ref, got_2_ref, got_ref, x3_ref, x2_ref, gains_ref, cot_ref, w0_ref, w1_ref, target_ref, q_ref,
    own_ref, peer_ref, col_ref, slot_ref, low3_ref, g2_ref, dq_ref, dkv_own_ref, dkv_peer_ref,
    gain_ref,
):
    halves = (w0_ref, w1_ref)
    rows = x3_ref.shape[0]
    grad_n3 = got_ref[...].astype(F32) + sum(
        ref[0:rows, :].astype(F32) for ref in (lo_ref, got_c_ref, got_2_ref)
    )
    grad_in, gain_3 = norm_back(x3_ref[...], gains_ref[2:3, :], grad_n3)
    grad_3 = cot_ref[...].astype(F32) + grad_in
    low3_ref[...] = grad_3.astype(BF16)
    grad = to_natural(low3_ref[...], halves, target_ref, 3 * INNER, INNER)
    reach = col_ref[...] == jnp.concatenate([slot_ref[k : k + 1, :] for k in range(2)], axis=1)
    rows = x3_ref.shape[0]
    slots = own_ref.shape[0]
    for pair in range(PAIRS):
        at = pair * LANES
        query = q_ref[:, at : at + LANES]
        key, value = key_value(own_ref, peer_ref, at)
        g_pair = grad[:, at : at + LANES]
        dq, dk, dv = [], [], []
        for side in range(2):
            probs = softmax(jnp.where(reach, dot_nt(pick(query, side), key), MASKED))
            dp = dot_nt(pick(g_pair, side), value)
            ds = (probs * (dp - jnp.sum(probs * dp, axis=-1, keepdims=True))).astype(BF16)
            dq.append(dot_nn(ds, key))
            dk.append(dot_tn(ds, query))
            dv.append(dot_tn(probs.astype(BF16), g_pair))
        dq_ref[:, at : at + LANES] = jnp.where(lane_half(rows, 0), dq[0], dq[1]).astype(BF16)
        left = lane_half(2 * slots, 0)
        for k, two in ((0, dk), (INNER, dv)):
            both = jnp.where(left, two[0], two[1]).astype(BF16)
            dkv_own_ref[:, k + at : k + at + LANES] = both[:slots]
            dkv_peer_ref[:, k + at : k + at + LANES] = both[slots:]
    back = from_natural(dq_ref[...], halves, target_ref, 0)
    grad_in, gain_2 = norm_back(x2_ref[...], gains_ref[1:2, :], back)
    g2_ref[...] = grad_3 + grad_in
    gain_ref[0:1, :] = gain_2
    gain_ref[1:2, :] = gain_3


def weights_kernel(
    dq_ref, low_ref, own_ref, peer_ref, low1_ref, n2_ref, low3_ref, mem_own_ref, mem_peer_ref, g2_ref,
    target_ref, one_ref, *out_refs,
):
    right = jnp.concatenate([n2_ref[...], low3_ref[...], mem_own_ref[...], mem_peer_ref[...]], axis=0)
    right_out = g2_ref[...].astype(BF16)
    for i, out_ref in enumerate(out_refs):

        def spread(order_ref, first, value):
            size = order_ref.shape[1] // 2
            hot = rows_of(order_ref, i * size, size, first, value.shape[1])
            return dot_nn(value, hot).astype(BF16)

        left = jnp.concatenate(
            [
                spread(target_ref, 0, dq_ref[...]),
                spread(target_ref, 3 * INNER, low_ref[...]),
                spread(target_ref, INNER, own_ref[...]),
                spread(target_ref, INNER, peer_ref[...]),
            ],
            axis=0,
        )
        cross = dot_tn(left, right).astype(BF16)
        out = dot_tn(spread(one_ref, 0, low1_ref[...]), right_out).astype(BF16)
        wide, slim = cross.shape[0] // 4, out.shape[0] // 4
        for k in range(4):
            at = k * (wide + slim)
            out_ref[at : at + wide, :] = cross[k * wide : (k + 1) * wide]
            out_ref[at + wide : at + wide + slim, :] = out[k * slim : (k + 1) * slim]


def columns_kernel(at_ref, held_ref, lo_ref, hi_ref, out_ref):
    rows = held_ref.shape[2]
    total = None
    for k in range(8):
        right = (lo_ref if k < 4 else hi_ref)[(k % 4) * rows : (k % 4 + 1) * rows, :]
        term = dot_nn(held_ref[at_ref[k]], right)
        total = term if total is None else total + term
    out_ref[...] = total.astype(BF16)


def assemble(parts, whole_ref):
    cols = parts[0].shape[0]
    for i, part in enumerate(parts):
        whole_ref[i * cols : (i + 1) * cols, :] = part[...]


def grad_hidden_kernel(c_ref, *refs):
    parts, out_ref, wd_ref = refs[:-2], refs[-2], refs[-1]
    assemble(parts, wd_ref)
    out_ref[...] = dot_nt(c_ref[...], wd_ref[...])


def ffn_kernel(n_ref, gh_ref, *refs):
    parts, (h_ref, dg_ref, du_ref, gn_ref, wg_ref, wu_ref) = refs[:-6], refs[-6:]
    assemble(parts[: len(parts) // 2], wg_ref)
    assemble(parts[len(parts) // 2 :], wu_ref)
    n = n_ref[...]
    gate = dot_nt(n, wg_ref[...])
    up = dot_nt(n, wu_ref[...])
    square = gate * gate
    t = jnp.tanh(GELU_A * gate * (1.0 + GELU_B * square))
    half = 0.5 * (1.0 + t)
    act = gate * half
    h_ref[...] = (act * up).astype(BF16)
    gh = gh_ref[...]
    slope = half + 0.5 * gate * (1.0 - t * t) * (GELU_A * (1.0 + 3.0 * GELU_B * square))
    d_gate = (gh * up * slope).astype(BF16)
    d_up = (gh * act).astype(BF16)
    dg_ref[...] = d_gate
    du_ref[...] = d_up
    gn_ref[...] = (dot_nn(d_gate, wg_ref[...]) + dot_nn(d_up, wu_ref[...])).astype(BF16)


def ffn_out_kernel(h_ref, *refs):
    parts, out_ref, wd_ref = refs[:-2], refs[-2], refs[-1]
    got_ref, parts = (parts[0], parts[1:]) if len(parts) % 2 else (None, parts)
    assemble(parts, wd_ref)
    value = dot_nn(h_ref[...], wd_ref[...])
    if got_ref is not None:
        value = value + got_ref[...].astype(F32)
    out_ref[...] = value.astype(BF16)


def ffn_weights_kernel(
    h0_ref, h1_ref, g0_ref, g1_ref, u0_ref, u1_ref, n0_ref, n1_ref, c0_ref, c1_ref, *out_refs
):
    sets = (
        ((h0_ref, c0_ref), (h1_ref, c1_ref)),
        ((g0_ref, n0_ref), (g1_ref, n1_ref)),
        ((u0_ref, n0_ref), (u1_ref, n1_ref)),
    )
    for out_ref, pairs in zip(out_refs, sets):
        out_ref[...] = sum(dot_tn(left[...], right[...]) for left, right in pairs).astype(BF16)


def on_device(
    tokens,
    memory,
    target_lengths,
    memory_lengths,
    keep_mask,
    distance_bucket_lookup,
    self_query,
    self_kv,
    self_out,
    cross_query,
    cross_key_value,
    cross_out,
    ffn_in,
    ffn_down,
    norm_gains,
    rel_bias,
    cotangent,
):
    size = {axis: lax.axis_size(axis) for axis in AXES}
    me = {axis: lax.axis_index(axis) for axis in AXES}
    rows, width = tokens.shape
    slots = memory.shape[0]
    part_rows, ff_rows = self_out.shape[0], ffn_down.shape[0]
    n_o = size["o"]
    quads = 2 * n_o

    def cut(value):
        if value.ndim < 2 or value.shape[-2] % LANES:
            return value
        return value.reshape(*value.shape[:-2], -1, LANES // 2, value.shape[-1])

    def permute(value, move):
        pairs = []
        for flat in range(quads * 8):
            rest, at = flat, {}
            for axis in reversed(AXES):
                at[axis], rest = rest % size[axis], rest // size[axis]
            to = move(dict(at))
            there = 0
            for axis in AXES:
                there = there * size[axis] + to[axis]
            pairs.append((flat, there))
        return lax.ppermute(cut(value), AXES, pairs).reshape(value.shape)

    def flips(**masks):
        def move(at):
            return {axis: at[axis] ^ masks.get(axis, 0) for axis in AXES}

        return move

    def flip_by_core(first, second):
        def move(at):
            at[first if at["c"] == 0 else second] ^= 1
            return at

        return move

    first_move, second_move = flip_by_core("b", "a"), flip_by_core("a", "b")
    core_move, peer_move = flips(c=1), flips(m=1)

    def grow(held, move):
        return jnp.concatenate([held, permute(held, move)], axis=0)

    def exchange(value, axes, parts):
        value = value.reshape(parts, -1, value.shape[-1])
        got = lax.all_to_all(cut(value), axes, split_axis=0, concat_axis=0, tiled=True)
        return got.reshape(value.shape)

    stage = lax.optimization_barrier
    full, slim = (rows, width), (rows, INNER)
    half, cols = 4 * rows, quads * ff_rows
    kv_shape = shape(slots, 2 * INNER)
    down, gate, up = (pltpu.VMEM((cols, width), BF16) for _ in range(3))

    def flat_of(at):
        return ((((at["o"] * 2 + at["a"]) * 2 + at["b"]) * 2 + at["c"]) * 2) + at["m"]

    def mask_of(eighth, quad, core):
        by_1, by_2 = ("b", "a") if core ^ (eighth // 4) == 0 else ("a", "b")
        at = {"o": quad % n_o, "m": quad // n_o, "c": eighth // 4}
        at[by_1], at[by_2] = eighth % 2, (eighth // 2) % 2
        return flat_of(at)

    masks = np.array(
        [[mask_of(e, q, core) for e in range(8) for q in range(quads)] for core in range(2)]
    ).astype(np.int32)
    piece = 4 * part_rows

    def target_of(owner, padded):
        row = np.arange(padded)
        base = row // part_rows * INNER + row % part_rows
        return owner[:, None] * part_rows + base[None, :].astype(np.int32)

    moves = [flips(o=k % n_o, m=k // n_o) for k in range(1, quads)]
    wide = quads * piece

    own_both = kernel_call(
        shards_kernel, shape(2 * piece, width), self_query.T, jnp.transpose(self_kv, (2, 0, 1)), self_out,
        cross_query.T, jnp.transpose(cross_key_value, (2, 0, 1)), cross_out, us=2, fetch=True,
    )
    got = [own_both] + [permute(own_both, move) for move in moves]
    here, at_core = after((flat_of(me), me["c"]), own_both)
    mask = jnp.where(at_core == 0, masks[0], masks[1])
    target = target_of(here ^ mask, piece).reshape(1, -1)
    one = jnp.where(
        np.arange(16)[None, :] < part_rows, target_of(here ^ mask, 16), -1
    ).reshape(1, -1)
    om_bits = flat_of({"o": n_o - 1, "a": 0, "b": 0, "c": 0, "m": 1})
    quad_masks = masks[0, :quads]
    owner = (np.arange(8, dtype=np.int32)[:, None] * 2) | ((here & om_bits) ^ quad_masks)[None, :]
    plain = target_of(owner.reshape(-1), 40).reshape(1, -1)
    eight_at = ((here ^ mask[::quads]) // 2) % 8
    both = kernel_call(join_kernel, shape(2 * quads * piece, width), *got, us=1)
    cot_1 = grow(cotangent, first_move)
    keep = keep_mask.reshape(1, -1)
    peer_keep = permute(keep, peer_move)
    own_gate, own_up = jnp.swapaxes(ffn_in, 1, 2)

    def two_halves(held, got):
        half = held.shape[0] // 2
        return [jnp.concatenate([held[at : at + half], got[at : at + half]], axis=0) for at in (0, half)]

    both, cot_1, peer_keep, memory, target, one, plain, eight_at, own_down = stage(
        (both, cot_1, peer_keep, memory, target, one, plain, eight_at, ffn_down)
    )
    both = jnp.concatenate(two_halves(both, permute(both, first_move)), axis=0)
    peer_memory = permute(memory, peer_move)
    lookup = distance_bucket_lookup.reshape(1, -1)
    ring, items_col, items_row, slot, own_1 = kernel_call(
        tables_kernel,
        [
            shape(8, WIDTH, kind=F32), shape(rows, 1, kind=jnp.int32), shape(1, rows, kind=jnp.int32),
            shape(2, slots, kind=jnp.int32), shape(*full),
        ],
        me["m"].reshape(1), target_lengths[0], memory_lengths, keep, peer_keep, lookup, rel_bias,
        tokens, norm_gains, scalars=3,
    )

    def over_o(own):
        return [own] + [permute(own, flips(o=k)) for k in range(1, n_o)]

    def over_m(parts, own_m):
        return parts + [own_m] + [permute(v, peer_move) for v in parts[1:]]

    down_o, down_m = over_o(own_down), permute(own_down, peer_move)

    both, ring, own_1, own_gate, down_o, down_m = stage(
        (both, ring, own_1, own_gate, down_o, down_m)
    )
    self_lo, cross_lo = two_halves(both, permute(both, second_move))
    gate_o, gate_m = over_o(own_gate), permute(own_gate, peer_move)
    w_down = over_m(down_o, down_m)

    self_lo, cross_lo, peer_memory, gate_o, gate_m, target, w_down, own_up = stage(
        (self_lo, cross_lo, peer_memory, gate_o, gate_m, target, w_down, own_up)
    )
    up_o, up_m = over_o(own_up), permute(own_up, peer_move)
    w_self = (self_lo, permute(self_lo, core_move))
    w_cross = (cross_lo, permute(cross_lo, core_move))

    w_self, w_cross, cot_1, gate_o = stage((w_self, w_cross, cot_1, gate_o))
    x_2, n_2, qkv, low_1 = kernel_call(
        self_forward_kernel,
        [shape(*full, kind=F32), shape(*full), shape(rows, 3 * INNER), shape(*slim)],
        tokens, own_1, norm_gains, *w_self, target, ring, items_col, items_row,
    )
    kv_own, kv_peer = kernel_call(
        memory_forward_kernel, [kv_shape] * 2, memory, peer_memory, *w_cross, target
    )
    x_3, n_3, q_2, low_2 = kernel_call(
        cross_forward_kernel,
        [shape(*full, kind=F32), shape(*full), shape(*slim), shape(*slim)],
        x_2, n_2, norm_gains, *w_cross, target, kv_own, kv_peer, items_col, slot,
    )
    cot_lo = grow(cot_1, second_move)
    w_gate = over_m(gate_o, gate_m)

    x_3, n_3, cot_lo, w_gate, up_o, up_m = stage((x_3, n_3, cot_lo, w_gate, up_o, up_m))
    w_up = over_m(up_o, up_m)
    n_1 = grow(n_3, first_move)
    cot_hi = permute(cot_lo, core_move)

    def grad_hidden(value):
        return kernel_call(
            grad_hidden_kernel, shape(half, cols, kind=F32), value, *w_down, scratch=[down], us=2
        )

    gh_lo = grad_hidden(cot_lo)

    n_1, cot_hi, gh_lo, own_1 = stage((n_1, cot_hi, gh_lo, own_1))
    n_lo = grow(n_1, second_move)
    gh_hi = grad_hidden(cot_hi)

    def ffn(value, gh):
        return kernel_call(
            ffn_kernel,
            [shape(half, cols), shape(half, cols), shape(half, cols), shape(half, width)],
            value, gh, *w_gate, *w_up, scratch=[gate, up],
        )

    n_lo, gh_hi, own_1, w_up = stage((n_lo, gh_hi, own_1, w_up))
    n_hi = permute(n_lo, core_move)
    lo_f = ffn(n_lo, gh_lo)
    one_1 = grow(own_1, first_move)

    n_hi, lo_f = stage((n_hi, lo_f))
    hi_f = ffn(n_hi, gh_hi)

    (h_lo, g_lo, u_lo, gn_lo), (h_hi, g_hi, u_hi, gn_hi) = stage((lo_f, hi_f))
    got_c = permute(gn_hi, core_move)

    def ffn_out(*args):
        return kernel_call(
            ffn_out_kernel, shape(half, width), *args, *w_down, scratch=[down], us=2
        )

    out_hi = ffn_out(h_hi)

    def summed(at, end, *parts):
        return sum(v[at:end].astype(F32) for v in parts).astype(BF16)

    got_c, out_hi, h_lo = stage((got_c, out_hi, h_lo))
    got_2 = permute(summed(2 * rows, 4 * rows, gn_lo, got_c), second_move)
    out_got = permute(out_hi, core_move)
    grad_down, grad_gate, grad_up = kernel_call(
        ffn_weights_kernel,
        [shape(cols, width)] * 3,
        h_lo, h_hi, g_lo, g_hi, u_lo, u_hi, n_lo, n_hi, cot_lo, cot_hi,
    )

    got_2, out_got, grad_down = stage((got_2, out_got, grad_down))
    got_1 = permute(summed(rows, 2 * rows, gn_lo, got_c, got_2), first_move)
    out_lo = ffn_out(h_lo, out_got)

    def over_m_back(grad):
        return permute(grad[cols // 2 :], peer_move)

    def over_o_back(grad, got):
        return [
            permute(summed(k * ff_rows, (k + 1) * ff_rows, grad, got), flips(o=k))
            for k in range(1, n_o)
        ]

    def back_sum(part, *parts):
        return sum(v[:part].astype(F32) for v in parts)

    down_m = over_m_back(grad_down)

    got_1, out_lo, one_1 = stage((got_1, out_lo, one_1))
    low_3, grad_2, dq, dkv_own, dkv_peer, gains_23 = kernel_call(
        cross_backward_kernel,
        [
            shape(*full), shape(*full, kind=F32), shape(*slim), kv_shape, kv_shape,
            shape(2, width, kind=F32),
        ],
        gn_lo, got_c, got_2, got_1, x_3, x_2, norm_gains, cotangent, *w_cross, target, q_2, kv_own,
        kv_peer, items_col, slot, us=8,
    )
    n1_lo = grow(one_1, second_move)

    grad_2, dq, down_m, grad_gate, dkv_peer = stage((grad_2, dq, down_m, grad_gate, dkv_peer))
    grad_tokens, dyt, small = kernel_call(
        self_backward_kernel,
        [shape(*full, kind=F32), shape(8 * quads * 40, rows), shape(4, width, kind=F32)],
        grad_2, tokens, norm_gains, *w_self, target, plain, qkv, ring, items_col, items_row, lookup,
        gains_23, scratch=[pltpu.VMEM((rows, 3 * INNER), BF16), pltpu.VMEM((8, WIDTH), F32)], us=8,
    )
    gate_m = over_m_back(grad_gate)

    grad_tokens, dyt, small, n1_lo, down_m = stage((grad_tokens, dyt, small, n1_lo, down_m))
    held = exchange(dyt, GROUP, 8)
    stack = shape(4 * quads * (piece + 16), width)
    kept, sent = kernel_call(
        weights_kernel, [stack] * 2,
        dq, low_2, dkv_own, dkv_peer, low_1, n_2, low_3, memory, peer_memory, grad_2, target, one, us=10,
    )
    n1_hi = permute(n1_lo, core_move)
    small = small + permute(small, core_move)
    down_b = over_o_back(grad_down, down_m)
    out_2 = permute(out_lo[2 * rows :], second_move)

    held, sent, small, n1_hi, gate_m, grad_up, out_2, dkv_peer, down_b = stage(
        (held, sent, small, n1_hi, gate_m, grad_up, out_2, dkv_peer, down_b)
    )
    cross_c = permute(sent, core_move)
    part_self = kernel_call(
        columns_kernel, shape(quads * 40, width), eight_at, held, n1_lo, n1_hi, scalars=1, us=2
    )
    self_got = [permute(part_self[k * 40 + 40 : k * 40 + 80], move) for k, move in enumerate(moves)]
    small = small + permute(small, second_move)
    out_1 = permute(summed(rows, 2 * rows, out_lo, out_2), first_move)
    up_m = over_m_back(grad_up)
    dkv_got = permute(dkv_peer, peer_move)

    cross_c, part_self, small, gate_m, dkv_got, out_1 = stage(
        (cross_c, part_self, small, gate_m, dkv_got, out_1)
    )
    gate_b = over_o_back(grad_gate, gate_m)
    block_out = summed(0, rows, x_3, out_lo, out_2, out_1)
    quarter = kept.shape[0] // 4
    cross_2 = permute(summed(2 * quarter, 4 * quarter, kept, cross_c), second_move)
    small = small + permute(small, first_move)
    sum_down = back_sum(ff_rows, grad_down, down_m, *down_b)

    cross_2, self_got, small, up_m, dkv_got, sum_down, block_out, gate_b = stage(
        (cross_2, self_got, small, up_m, dkv_got, sum_down, block_out, gate_b)
    )
    sum_gate = back_sum(ff_rows, grad_gate, gate_m, *gate_b)
    cross_1 = permute(summed(quarter, 2 * quarter, kept, cross_c, cross_2), first_move)
    small_got = [permute(small, move) for move in moves]
    up_b = over_o_back(grad_up, up_m)
    grad_memory = kernel_call(
        memory_backward_kernel, shape(slots, width, kind=F32), dkv_own, dkv_got, *w_cross, target
    )
    sum_self = back_sum(40, part_self, *self_got)

    cross_1, small_got, sum_self, grad_memory, sum_gate = stage(
        (cross_1, small_got, sum_self, grad_memory, sum_gate)
    )

    def pieces(k):
        return jnp.concatenate(
            [
                sum(v[at:end].astype(F32) for v in (kept, cross_c, cross_2, cross_1))
                for at, end in ((k * piece, k * piece + piece), (wide + k * 16, wide + k * 16 + 16))
            ],
            axis=0,
        )

    pieces_got = [permute(pieces(k + 1).astype(BF16), move) for k, move in enumerate(moves)]
    small = small + sum(small_got)

    pieces_got, up_b, small = stage((pieces_got, up_b, small))
    sum_cross = pieces(0) + sum(g.astype(F32) for g in pieces_got)
    sum_up = back_sum(ff_rows, grad_up, up_m, *up_b)

    def three(total):
        query, key, value = (total[k * part_rows : (k + 1) * part_rows] for k in range(3))
        return query.T, jnp.transpose(jnp.stack([key, value], axis=1), (1, 2, 0))

    squery, skv = three(sum_self)
    cquery, ckv = three(sum_cross)
    fin = jnp.swapaxes(jnp.stack([sum_gate, sum_up]), 1, 2)
    base = 4 * part_rows
    return (
        block_out,
        grad_tokens,
        grad_memory,
        squery,
        skv,
        sum_cross[base : base + part_rows],
        cquery,
        ckv,
        sum_cross[3 * part_rows : base],
        fin,
        sum_down,
        small[:3],
        small[3, : HEADS * LANES].reshape(HEADS, LANES)[:, : rel_bias.shape[0]].T,
    )


def solution(mesh):
    n_tok, n_mem = mesh.devices.shape
    grid = Mesh(mesh.devices.reshape(n_tok // 8, 2, 2, 2, n_mem), AXES)
    tok = AXES[:-1]
    rows = P(AXES, None)
    cols = P(None, AXES)
    deep = P(None, None, AXES)
    in_specs = (
        rows,
        rows,
        P(tok, None, None),
        P(tok, None),
        P(AXES),
        P(),
        cols,
        deep,
        rows,
        cols,
        deep,
        rows,
        deep,
        rows,
        P(),
        P(),
        rows,
    )
    out_specs = (rows, rows, rows, cols, deep, rows, cols, deep, rows, deep, rows, P(), P())
    return jax.shard_map(
        on_device, mesh=grid, in_specs=in_specs, out_specs=out_specs, check_vma=False
    )
```
